256 devices in a mesh: seq: 64 (over z, y, core), mp: 4 (over x).
Axes of the slice: x: 4, y: 4, z: 8, core: 2. Of those that a mesh axis runs over, the one named last changes fastest.
Arguments:
- tokens: bfloat16 [1, 16384, 768], P(None, 'seq'), may hold values from -16 to 16
- w_qkv: bfloat16 [3, 768, 768], P(None, 'mp'), may hold values from -0.21875 to 0.21875
- w_out: bfloat16 [768, 768], P('mp'), may hold values from -0.21875 to 0.21875
- grad_y: bfloat16 [1, 16384, 768], P(None, 'seq'), may hold values from -16 to 16
Outputs:
- mixed: bfloat16 [1, 16384, 768], P(None, 'seq', 'mp')
- grad_tokens: bfloat16 [1, 16384, 768], P(None, 'seq', 'mp')
- grad_wqkv: float32 [768, 3, 768], P('seq', None, 'mp')
- grad_wout: float32 [768, 768], P('seq', 'mp')
The draws below stay inside these ranges and needn't reach their ends.
All inputs are finite; a program needn't handle non-finite values.
Results may differ from the reference program's by a relative error of at most 0.029.
Values may be sent and summed in bfloat16 or wider, within the bound.
A program may use at most 64 MiB of HBM per device.

```python
import math
from functools import partial
import jax
import jax.numpy as jnp
from jax import lax

D = 768
HEAD = 64
BLOCK = 128
LEVELS = 4
SEQS = 1
LEN = 16384


def raised(values, stream_key, source, target, blocks, factor):
    owner, partner = [(jnp.arange(values.shape[position]) // (values.shape[position] // blocks)).reshape([-1 if axis == position else 1 for axis in range(values.ndim)]) for position in (source, target)]
    chosen = jax.random.permutation(stream_key, blocks)[partner]
    strong = (owner == chosen) | (owner == (partner + blocks // 2) % blocks)
    return jnp.where(strong, factor * values, values)


def block_scale(key, shape, pieces, least, largest):
    def one(axis_at, shards_of):
        heights = jax.random.uniform(jax.random.fold_in(jax.random.fold_in(key, 6), axis_at), (shards_of,), jnp.float32, least / len(pieces), largest / len(pieces))
        return jnp.repeat(jnp.exp(heights), shape[axis_at] // shards_of).reshape((-1,) + (1,) * (len(shape) - axis_at - 1))

    loudness = one(*pieces[0])
    for cut in pieces[1:]:
        loudness = loudness * one(*cut)
    return loudness


def normal_values(rng, dims, spread, bound, split=(), dtype=jnp.bfloat16):
    drawn = spread * jax.random.normal(rng, dims, jnp.float32)
    if split:
        drawn = drawn * block_scale(rng, dims, split, -0.22, 0.18)
    return jnp.clip(drawn, -bound, bound).astype(dtype)


def gaussian_with(key, shape, spread, most, split, heavy, held_as=jnp.bfloat16):
    values = spread * jax.random.normal(key, shape, jnp.float32)
    if split:
        values = values * block_scale(key, shape, split, -0.22, 0.18)
    return jnp.clip(raised(values, jax.random.fold_in(key, 3), *heavy), -most, most).astype(held_as)


def setup_inputs(seed: int = 0) -> dict:
    keys = jax.random.split(jax.random.key(seed), 5)
    return {
        "tokens": gaussian_with(keys[0], (SEQS, LEN, D), 1.0, 16.0, ((1, 64),), (1, 2, 64, 4.0)),
        "w_qkv": normal_values(keys[1], (3, D, D), D ** -0.5, 0.21875, ((1, 4),)),
        "w_out": normal_values(keys[2], (D, D), D ** -0.5, 0.21875, ((0, 4),)),
        "grad_y": gaussian_with(keys[3], (SEQS, LEN, D), 1.0, 16.0, ((1, 64),), (1, 2, 64, 4.0)),
    }


SCORE_SCALE = 32.0
NORM_EPSILON = 1e-06
ROOT_HALF = 0.7071067811865476
PAD_BLOCKS = 3
NEAR_OFFSETS = (-3, -2, -1, 0, 1, 2, 3)
NEAR_EVEN_KEEP = (0.0, 1.0, 1.0, 1.0, 1.0, 1.0, 1.0)
NEAR_ODD_KEEP = (1.0, 1.0, 1.0, 1.0, 1.0, 1.0, 0.0)
FAR_OFFSETS = (-3, -2, 2, 3)
EVEN_KEEP = (0.0, 1.0, 1.0, 1.0)
ODD_KEEP = (1.0, 1.0, 1.0, 0.0)

def unit_rows(vector):
    return vector * lax.rsqrt(lax.optimization_barrier(jnp.mean(vector * vector, axis=-1, keepdims=True)) + NORM_EPSILON)

def pair_rows(vector):
    extent = vector.shape
    return vector.reshape(extent[0], extent[1] // 2, 2, extent[2], extent[3])

def pyramid(query_pre, key_pre, value_pre):
    query_float = unit_rows(query_pre)
    key_float = unit_rows(key_pre)
    value_float = value_pre
    levels_out = []
    for level_index in range(LEVELS):
        if level_index > 0:
            query_float = unit_rows(lax.optimization_barrier(jnp.mean(pair_rows(query_float), axis=2)))
            key_float = unit_rows(lax.optimization_barrier(jnp.mean(pair_rows(key_float), axis=2)))
            value_float = lax.optimization_barrier(jnp.sum(pair_rows(value_float), axis=2)) * ROOT_HALF
        levels_out.append((query_float.astype(jnp.bfloat16), key_float.astype(jnp.bfloat16), value_float.astype(jnp.bfloat16)))
    return tuple(levels_out)

def pool_total(values_in, factor):
    extent = values_in.shape
    return lax.optimization_barrier(jnp.sum(values_in.reshape((extent[0], extent[1] // factor, factor) + extent[2:]), axis=2))

def rounded(values_in):
    return lax.optimization_barrier(values_in.astype(jnp.bfloat16)).astype(jnp.float32)

def visible(level_index, blocks):
    if level_index == 0:
        offsets, even_keep, odd_keep = (NEAR_OFFSETS, NEAR_EVEN_KEEP, NEAR_ODD_KEEP)
    else:
        offsets, even_keep, odd_keep = (FAR_OFFSETS, EVEN_KEEP, ODD_KEEP)
    block_ids = jnp.arange(blocks)[:, None]
    moved = block_ids + jnp.array(offsets)[None, :]
    keep_mask = ((moved >= 0) & (moved < blocks)).astype(jnp.float32)
    parity = jnp.where(block_ids % 2 == 0, jnp.array(even_keep, jnp.float32)[None, :], jnp.array(odd_keep, jnp.float32)[None, :])
    keep_mask = keep_mask * parity
    return (offsets, jnp.repeat(keep_mask, BLOCK, axis=1))

def windows(blocked, offsets):
    block_count = blocked.shape[0]
    padded = jnp.pad(blocked, ((PAD_BLOCKS, PAD_BLOCKS),) + ((0, 0),) * (blocked.ndim - 1))
    return jnp.concatenate([padded[PAD_BLOCKS + offset:PAD_BLOCKS + offset + block_count] for offset in offsets], axis=1)

def unwindows(window_grad, offsets):
    block_count = window_grad.shape[0]
    total = jnp.zeros((block_count, BLOCK) + window_grad.shape[2:], jnp.float32)
    for slot_index, offset in enumerate(offsets):
        grad_piece = window_grad[:, slot_index * BLOCK:(slot_index + 1) * BLOCK]
        padded = jnp.pad(grad_piece, ((PAD_BLOCKS, PAD_BLOCKS),) + ((0, 0),) * (grad_piece.ndim - 1))
        total = total + padded[PAD_BLOCKS - offset:PAD_BLOCKS - offset + block_count]
    return total

def level_weights(query_rows, key_rows, value_rows, level_index):
    head_count = query_rows.shape[1]
    block_count = query_rows.shape[0] // BLOCK
    offsets, column_keep = visible(level_index, block_count)
    query_blocks = query_rows.reshape(block_count, BLOCK, head_count, HEAD).astype(jnp.float32)
    key_windows = windows(key_rows.reshape(block_count, BLOCK, head_count, HEAD), offsets).astype(jnp.float32)
    value_windows = windows(value_rows.reshape(block_count, BLOCK, head_count, HEAD), offsets).astype(jnp.float32)
    scores = jnp.einsum('bihe,bjhe->bhij', query_blocks, key_windows) * (SCORE_SCALE / HEAD)
    weights = jnp.exp(scores) * (float(2 ** level_index) * column_keep[:, None, None, :])
    return (offsets, query_blocks, key_windows, value_windows, weights)

def level_forward(packed, level_index):
    query_rows, key_rows, value_rows = packed
    head_count = query_rows.shape[1]
    offsets, query_blocks, key_windows, value_windows, weights = level_weights(query_rows, key_rows, value_rows, level_index)
    numer_level = jnp.einsum('bhij,bjhe->bihe', rounded(weights), value_windows)
    denom_level = jnp.swapaxes(lax.optimization_barrier(jnp.sum(weights, axis=-1)), 1, 2)
    return (numer_level.reshape(-1, head_count, HEAD), denom_level.reshape(-1, head_count))

def level_backward(packed, level_index):
    query_rows, key_rows, value_rows, pulled, offset_sum = packed
    head_count = query_rows.shape[1]
    block_count = query_rows.shape[0] // BLOCK
    offsets, query_blocks, key_windows, value_windows, weights = level_weights(query_rows, key_rows, value_rows, level_index)
    pulled_low = rounded(pulled).reshape(block_count, BLOCK, head_count, HEAD)
    inner_dots = jnp.einsum('bihe,bjhe->bhij', pulled_low, value_windows)
    centred = jnp.swapaxes(offset_sum.reshape(block_count, BLOCK, head_count), 1, 2)[..., None]
    slopes = rounded(weights * (inner_dots - centred) * (SCORE_SCALE / HEAD))
    d_query = jnp.einsum('bhij,bjhe->bihe', slopes, key_windows)
    d_key = unwindows(jnp.einsum('bhij,bihe->bjhe', slopes, query_blocks), offsets)
    d_value = unwindows(jnp.einsum('bhij,bihe->bjhe', rounded(weights), pulled_low), offsets)
    return (d_query.reshape(-1, head_count, HEAD), d_key.reshape(-1, head_count, HEAD), d_value.reshape(-1, head_count, HEAD))

def reference(tokens, w_qkv, w_out, grad_y):
    seq_count, length, model_width = tokens.shape
    head_count = model_width // HEAD
    flat_tokens = tokens.reshape(seq_count * length, model_width)
    w_matrix = jnp.transpose(w_qkv, (2, 0, 1)).reshape(model_width, 3 * model_width)
    projected = jnp.dot(flat_tokens, w_matrix, preferred_element_type=jnp.float32)
    projected = projected.reshape(seq_count, length, 3, head_count, HEAD)
    levels_out, pull_back = jax.vjp(pyramid, projected[:, :, 0], projected[:, :, 1], projected[:, :, 2])
    numer = jnp.zeros((seq_count, length, head_count, HEAD), jnp.float32)
    denom = jnp.zeros((seq_count, length, head_count), jnp.float32)
    for level_index in range(LEVELS):
        numer_level, denom_level = lax.map(partial(level_forward, level_index=level_index), levels_out[level_index])
        numer = numer + jnp.repeat(numer_level, 2 ** level_index, axis=1)
        denom = denom + jnp.repeat(denom_level, 2 ** level_index, axis=1)
    attention = (numer / denom[..., None]).astype(jnp.bfloat16).reshape(seq_count * length, model_width)
    mixed = jnp.dot(attention, w_out, preferred_element_type=jnp.float32).astype(jnp.bfloat16)
    flat_grad = grad_y.reshape(seq_count * length, model_width)
    d_attention = jnp.dot(flat_grad, w_out.T, preferred_element_type=jnp.float32).astype(jnp.bfloat16)
    norm_scale = 1.0 / math.sqrt(seq_count * length)
    grad_wout = jnp.dot(flat_grad.T, attention, preferred_element_type=jnp.float32) * norm_scale
    attention_float = attention.astype(jnp.float32).reshape(seq_count, length, head_count, HEAD)
    d_attention_float = d_attention.astype(jnp.float32).reshape(seq_count, length, head_count, HEAD)
    inverse = 1.0 / denom
    pulled = d_attention_float * inverse[..., None]
    offset_sum = lax.optimization_barrier(jnp.sum(d_attention_float * attention_float, axis=-1)) * inverse
    cotangents = []
    for level_index in range(LEVELS):
        factor = 2 ** level_index
        query_rows, key_rows, value_rows = levels_out[level_index]
        d_query, d_key, d_value = lax.map(partial(level_backward, level_index=level_index), (query_rows, key_rows, value_rows, pool_total(pulled, factor), pool_total(offset_sum, factor)))
        cotangents.append((d_query.astype(jnp.bfloat16), d_key.astype(jnp.bfloat16), d_value.astype(jnp.bfloat16)))
    grads_pre = pull_back(tuple(cotangents))
    d_projected = jnp.stack(grads_pre, axis=2).astype(jnp.bfloat16).reshape(seq_count * length, 3 * model_width)
    grad_tokens = jnp.dot(d_projected, w_matrix.T, preferred_element_type=jnp.float32).astype(jnp.bfloat16)
    grad_wqkv = (jnp.dot(flat_tokens.T, d_projected, preferred_element_type=jnp.float32) * norm_scale).reshape(model_width, 3, model_width)
    return (mixed.reshape(seq_count, length, model_width), grad_tokens.reshape(seq_count, length, model_width), grad_wqkv, grad_wout)
```

```python
import jax
import jax.numpy as jnp
from jax import lax
from jax.experimental import pallas as pl
from jax.experimental.pallas import tpu as pltpu
from jax.sharding import PartitionSpec as P

F32 = jnp.float32
BF16 = jnp.bfloat16
MESH = pl.DeviceIdType.MESH
EPS = 1e-06
ROOT_HALF = 0.7071067811865476
NORM = 1.0 / 128.0
WINDOWS = (0, 128, 384, 512)


def nn(a, b):
    return jnp.dot(a, b, preferred_element_type=F32)


def nt(a, b):
    return lax.dot_general(a, b, (((1,), (1,)), ((), ())), preferred_element_type=F32)


def unit_parts(x):
    heads = x.reshape(x.shape[0] // 64, 64, x.shape[1])
    scale = lax.rsqrt(jnp.mean(heads * heads, axis=1, keepdims=True) + EPS)
    return heads * scale, scale


def unit(x):
    return unit_parts(x)[0].reshape(x.shape)


def unit_back(x, grad):
    y, scale = unit_parts(x)
    dy = grad.reshape(y.shape)
    return (scale * (dy - y * jnp.mean(y * dy, axis=1, keepdims=True))).reshape(x.shape)


def round_low(x):
    return x.astype(BF16).astype(F32)


def iota(shape, dim):
    return lax.broadcasted_iota(jnp.int32, shape, dim)


def one_hot(cond):
    return jnp.where(cond, 1.0, 0.0).astype(BF16)


def natural_token(row):
    high = row >> 5
    return (row & 31) * 8 + (((high & 1) << 2) | (high & 2) | ((high >> 2) & 1))


def kernel(
    tok_ref, wqkv_ref, wout_ref, gy_ref,
    mixed_ref, gt_ref, oa_ref, ob_ref,
    permt, u0, uc, kv0, kvc, ownc, kvt0, kvtc, w0, wc, qm0, qmc, gm0, gmc, c0, cc,
    num0, numc, den0, denc, dot_s, att_s, dq0, dqc, down, dsend0, dsendc, ret0, retc,
    tg, ptg, ra, pra, dkvt, pdkvt, mixs, mixr, gtacc, gts, gtr,
    gf, gs, yr, zs, zr,
    fs_sem, fr_sem, bs_sem, br_sem, cs_sem, cr_sem, ms_sem, mr_sem, ys_sem, yr_sem, zs_sem, zr_sem,
):
    s = lax.axis_index("seq")
    m = lax.axis_index("mp")
    core = lax.rem(s, 2)
    y = lax.rem(s // 2, 4)
    z = s // 8
    position = (s, s // 2, s // 4)
    extent = (64, 32, 16)
    skip = [3 - 6 * lax.rem(position[lv], 2) for lv in range(3)]

    def offset(lv, j):
        return (-2, 2, skip[lv])[j]

    def target(lv, j, part):
        block = lax.rem(position[lv] + offset(lv, j) + extent[lv], extent[lv])
        return block * (1 << lv) + part

    def back_slot(j):
        return (1, 0, 2)[j]

    prev_dev = lax.rem(s + 63, 64)
    next_dev = lax.rem(s + 1, 64)
    peer = s + 1 - 2 * core

    def y_dev(k):
        return z * 8 + lax.rem(y + k, 4) * 2 + core

    def z_dev(k):
        return lax.rem(z + k, 8) * 8 + y * 2 + core

    def mp_dev(k):
        return lax.rem(m + k, 4)

    barrier = pltpu.get_barrier_semaphore()
    partners = [{"seq": prev_dev}, {"seq": next_dev}]
    for lv in range(3):
        for j in range(3):
            for part in range(1 << lv):
                partners.append({"seq": target(lv, j, part)})
    partners += [{"seq": y_dev(k)} for k in range(1, 4)]
    partners += [{"seq": z_dev(k)} for k in range(1, 8)]
    partners += [{"mp": mp_dev(k)} for k in range(1, 4)]
    partners += [{"seq": peer}]
    for partner in partners:
        pl.semaphore_signal(barrier, inc=1, device_id=partner, device_id_type=MESH)

    def remote(src, dst, send, recv, where):
        return pltpu.make_async_remote_copy(
            src_ref=src, dst_ref=dst, send_sem=send, recv_sem=recv,
            device_id=where, device_id_type=MESH,
        )

    row = iota((256, 256), 0)
    col = iota((256, 256), 1)
    perm = one_hot(natural_token(row) == col)
    permt[...] = one_hot(natural_token(col) == row)
    tok_p = nn(perm, tok_ref[...]).astype(BF16)
    u0[...] = nt(wqkv_ref[...], tok_p)

    def store_q(dst, q_rows, n):
        dst[...] = jnp.zeros(dst.shape, BF16)
        half = (q_rows * 0.5).astype(BF16)
        for h in range(3):
            dst[64 * h : 64 * h + 64, h * n : h * n + n] = half[64 * h : 64 * h + 64]

    qk = unit(u0[0:384, :])
    v = u0[384:576, :]
    store_q(qm0, qk[0:192], 256)
    kv0[1] = jnp.concatenate([qk[192:384], v], axis=0).T.astype(BF16)
    for lv in range(3):
        if lv == 0:
            mean = (qk[:, 0:128] + qk[:, 128:256]) * 0.5
            v = (v[:, 0:128] + v[:, 128:256]) * ROOT_HALF
        else:
            mean = (qk + pltpu.roll(qk, 128 >> lv, 1)) * 0.5
            v = (v + pltpu.roll(v, 128 >> lv, 1)) * ROOT_HALF
        uc[lv] = mean
        qk = unit(mean)
        store_q(qmc.at[lv], qk[0:192], 128)
        ownc[lv] = jnp.concatenate([qk[192:384], v], axis=0).T.astype(BF16)

    pl.semaphore_wait(barrier, len(partners))

    for lv in range(3):
        rows = 128 >> lv
        mine = lax.rem(s, 1 << lv) * rows
        for j in range(3):
            i = 3 * lv + back_slot(j)
            for part in range(1 << lv):
                remote(
                    ownc.at[lv, pl.ds(0, rows)],
                    kvc.at[i, pl.ds(mine, rows)],
                    fs_sem.at[i], fr_sem.at[i], {"seq": target(lv, j, part)},
                ).start()
    remote(kv0.at[1], kv0.at[0], fs_sem.at[9], fr_sem.at[9], {"seq": next_dev}).start()
    remote(kv0.at[1], kv0.at[2], fs_sem.at[10], fr_sem.at[10], {"seq": prev_dev}).start()

    num0[...] = jnp.zeros(num0.shape, F32)
    numc[...] = jnp.zeros(numc.shape, F32)
    den0[...] = jnp.zeros(den0.shape, F32)
    denc[...] = jnp.zeros(denc.shape, F32)
    dq0[...] = jnp.zeros(dq0.shape, F32)
    dqc[...] = jnp.zeros(dqc.shape, F32)
    ra[...] = jnp.zeros(ra.shape, BF16)
    pra[0:192, 256:512] = jnp.zeros((192, 256), BF16)
    pra[192:384, 0:256] = jnp.zeros((192, 256), BF16)

    def forward(keys, keyst, qm, w_ref, num, den, factor, n):
        block = keys[...]
        count = block.shape[0]
        keyst[...] = block.astype(F32).T.astype(BF16)
        for h in range(3):
            lanes = slice(h * n, h * n + n)
            w = jnp.exp(nn(block[:, 0:256], qm[:, lanes])) * factor
            den[:, lanes] += jnp.sum(w.reshape(count // 8, 8, n), axis=0)
            wb = w.astype(BF16)
            w_ref[:, lanes] = wb
            num[64 * h : 64 * h + 64, :] += nn(keyst[192 + 64 * h : 256 + 64 * h, :], wb)

    def keep0(j):
        if j == 1:
            return jnp.float32(1.0)
        inside = s > 0 if j == 0 else s < 63
        return jnp.where(inside, jnp.float32(1.0), jnp.float32(0.0))

    forward(kv0.at[1], kvt0.at[1], qm0, w0.at[1], num0, den0, keep0(1), 256)

    gy_p = nn(perm, gy_ref[...]).astype(BF16)
    dot_s[...] = nt(wout_ref[...], gy_p).astype(BF16)
    for half in range(2):
        index = iota((384, 768), 0)
        twelfth = (index * 5462) >> 16
        feature = (twelfth & 7) * 96 + (twelfth >> 3) * 24 + half * 12 + (index - 12 * twelfth)
        pick = one_hot(feature == iota((384, 768), 1))
        tg[half, :, 0:256] = nt(pick, tok_p).astype(BF16)
        tg[half, :, 256:512] = nt(pick, gy_p).astype(BF16)
    remote(tg.at[1 - core], ptg, cs_sem.at[0], cr_sem.at[0], {"seq": peer}).start()

    def arrived(ref, sem, spare):
        remote(ref, ref, spare, sem, {"seq": peer}).wait_recv()

    def left(ref, sem, spare):
        remote(ref, ref, sem, spare, {"seq": peer}).wait_send()

    for lv in range(3):
        for j in range(3):
            i = 3 * lv + j
            place = position[lv] + offset(lv, j)
            inside = (place >= 0) & (place < extent[lv])
            factor = jnp.where(inside, jnp.float32(2 << lv), jnp.float32(0.0))
            arrived(kvc.at[i], fr_sem.at[i], fs_sem.at[i])
            forward(kvc.at[i], kvtc.at[i], qmc.at[lv], wc.at[i], numc, denc, factor, 128)
    for j in (0, 2):
        arrived(kv0.at[j], fr_sem.at[9 + j // 2], fs_sem.at[9 + j // 2])
        forward(kv0.at[j], kvt0.at[j], qm0, w0.at[j], num0, den0, keep0(j), 256)

    lane = iota((1, 128), 1)
    gm0[...] = jnp.zeros(gm0.shape, BF16)
    gmc[...] = jnp.zeros(gmc.shape, BF16)
    for h in range(3):
        rows = slice(64 * h, 64 * h + 64)
        grows = slice(64 * h + 64, 64 * h + 128)
        coarse = jnp.sum(denc[:, 128 * h : 128 * h + 128], axis=0, keepdims=True)
        den = jnp.sum(den0[:, 256 * h : 256 * h + 256], axis=0, keepdims=True)
        inverse = 1.0 / (den + jnp.concatenate([coarse, coarse], axis=1))
        more = numc[rows, :]
        att = ((num0[rows, :] + jnp.concatenate([more, more], axis=1)) * inverse).astype(BF16)
        ra[192 + 64 * h : 256 + 64 * h, 256:512] = att
        att_s[rows, :] = att
        d_att = dot_s[rows, :].astype(F32)
        g = d_att * inverse
        c = jnp.sum(d_att * att.astype(F32), axis=0, keepdims=True) * inverse
        gm0[grows, 256 * h : 256 * h + 256] = g.astype(BF16)
        c0[:, 256 * h : 256 * h + 256] = jnp.broadcast_to(c, (8, 256))
        g = g[:, 0:128] + g[:, 128:256]
        c = c[:, 0:128] + c[:, 128:256]
        for lv in range(3):
            if lv > 0:
                g = g + pltpu.roll(g, 128 >> lv, 1)
                c = c + pltpu.roll(jnp.broadcast_to(c, (8, 128)), 128 >> lv, 1)[0:1]
            used = lane < (128 >> lv)
            gmc[lv, grows, 128 * h : 128 * h + 128] = jnp.where(used, g, 0.0).astype(BF16)
            cc[lv, :, 128 * h : 128 * h + 128] = jnp.broadcast_to(
                jnp.where(used, c, 0.0), (8, 128)
            )
    remote(
        ra.at[pl.ds(192, 192), pl.ds(256, 256)], pra.at[pl.ds(192, 192), pl.ds(256, 256)],
        cs_sem.at[1], cr_sem.at[1], {"seq": peer},
    ).start()

    def backward(keys, keyst, qm, gm, c_rows, w_ref, dq, n):
        count = keys.shape[0]
        dk = jnp.zeros((count, 256), F32)
        dv = jnp.zeros((count, 256), F32)
        for h in range(3):
            lanes = slice(h * n, h * n + n)
            wb = w_ref[:, lanes]
            inner = nn(keys[:, 128:384], gm[:, lanes])
            slope = (wb.astype(F32) * (inner - c_rows[0:1, lanes])).astype(BF16)
            dq[64 * h : 64 * h + 64, :] += nn(keyst[64 * h : 64 * h + 64, :], slope)
            dk += nt(slope, qm[:, lanes])
            dv += nt(wb, gm[:, lanes])
        return jnp.concatenate(
            [dk[:, 0:128], dk[:, 128:256] + dv[:, 0:128], dv[:, 128:256]], axis=1
        )

    for lv in (2, 1, 0):
        rows = 128 >> lv
        mine = lax.rem(s, 1 << lv) * rows
        for j in range(3):
            i = 3 * lv + j
            k = 3 * lv + back_slot(j)
            dsendc[i] = backward(
                kvc.at[i], kvtc.at[i], qmc.at[lv], gmc.at[lv], cc.at[lv], wc.at[i], dqc.at[lv], 128
            ).astype(BF16)
            for part in range(1 << lv):
                remote(
                    dsendc.at[i, pl.ds(part * rows, rows)],
                    retc.at[k, pl.ds(mine, rows)],
                    bs_sem.at[k], br_sem.at[k], {"seq": target(lv, j, part)},
                ).start()
    for j in (0, 2):
        dsend0[j // 2] = backward(
            kv0.at[j], kvt0.at[j], qm0, gm0, c0, w0.at[j], dq0, 256
        ).astype(BF16)
        k = 1 - j // 2
        remote(
            dsend0.at[j // 2], ret0.at[k], bs_sem.at[9 + k], br_sem.at[9 + k],
            {"seq": prev_dev if j == 0 else next_dev},
        ).start()
    down[...] = backward(kv0.at[1], kvt0.at[1], qm0, gm0, c0, w0.at[1], dq0, 256)

    def spread(grad, lv):
        if lv == 0:
            return jnp.concatenate([grad, grad], axis=1)
        return grad + pltpu.roll(grad, 128 >> lv, 1)

    grad = round_low(dqc[2] * 0.5)
    for lv in (2, 1, 0):
        grad = unit_back(uc[lv, 0:192, :], grad) * 0.5
        base = dqc[lv - 1] if lv > 0 else dq0[...]
        grad = round_low(base * 0.5) + spread(grad, lv)
    dq_t = unit_back(u0[0:192, :], grad).astype(BF16)
    ra[0:192, 0:256] = dq_t
    remote(
        ra.at[pl.ds(0, 192), pl.ds(0, 256)], pra.at[pl.ds(0, 192), pl.ds(0, 256)],
        cs_sem.at[2], cr_sem.at[2], {"seq": peer},
    ).start()

    def column_parts(left_rows, weight, emit):
        for j in range(4):
            emit(j, nn(left_rows, weight[:, WINDOWS[j] : WINDOWS[j] + 256]))

    def own_columns(j, total):
        if j % 2 == 1:
            total = pltpu.roll(total, 192, 1)
        return total[:, 0:192].astype(BF16)

    def emit_mixed(j, total):
        mixs[j] = own_columns(j, total)

    column_parts(nt(permt[...], att_s[...]).astype(BF16), wout_ref, emit_mixed)
    for k in range(1, 4):
        remote(
            mixs.at[mp_dev(k)], mixr.at[k - 1], ms_sem.at[k - 1], mr_sem.at[k - 1],
            {"mp": mp_dev(k)},
        ).start()

    def emit_first(j, total):
        gtacc[j] = total

    column_parts(nt(permt[...], dq_t).astype(BF16), wqkv_ref.at[pl.ds(0, 192)], emit_first)

    def y_stage(r, total):
        gf[r] = total
        gs[r] = total.astype(BF16)
        for k in range(1, 4):
            remote(
                gs.at[r, pl.ds(lax.rem(y + k, 4) * 96, 96)], yr.at[r, k - 1],
                ys_sem.at[3 * r + k - 1], yr_sem.at[3 * r + k - 1], {"seq": y_dev(k)},
            ).start()

    at16 = iota((128, 96), 0)
    widen = one_hot(
        ((at16 >> 4) * 12 + (at16 & 15) == iota((128, 96), 1)) & ((at16 & 15) < 12)
    )

    def z_stage(r):
        total = gf[r, pl.ds(y * 96, 96), :]
        for k in range(3):
            arrived(yr.at[r, k], yr_sem.at[3 * r + k], ys_sem.at[3 * r + k])
            total += yr[r, k].astype(F32)
        zs[r] = nn(widen, total.astype(BF16)).astype(BF16)
        for k in range(1, 8):
            remote(
                zs.at[r, pl.ds(lax.rem(z + k, 8) * 16, 16)], zr.at[r, k - 1],
                zs_sem.at[7 * r + k - 1], zr_sem.at[7 * r + k - 1], {"seq": z_dev(k)},
            ).start()

    def z_finish(r, out):
        total = zs[r, pl.ds(z * 16, 16), :].astype(F32)
        for k in range(7):
            arrived(zr.at[r, k], zr_sem.at[7 * r + k], zs_sem.at[7 * r + k])
            total += zr[r, k].astype(F32)
        out[...] = total * NORM

    arrived(ptg, cr_sem.at[0], cs_sem.at[0])
    arrived(pra.at[pl.ds(192, 192), pl.ds(256, 256)], cr_sem.at[1], cs_sem.at[1])
    arrived(pra.at[pl.ds(0, 192), pl.ds(0, 256)], cr_sem.at[2], cs_sem.at[2])
    y_stage(0, nt(tg[core], ra[...]) + nt(ptg[...], pra[...]))

    def received(lv):
        rows = 128 >> lv
        total = jnp.zeros((rows, 384), F32)
        for j in range(3):
            i = 3 * lv + j
            arrived(retc.at[i], br_sem.at[i], bs_sem.at[i])
            for part in range(1 << lv):
                total += retc[i, part * rows : part * rows + rows, :].astype(F32)
        total = round_low(total)
        if lv > 0:
            total = jnp.concatenate([total, jnp.zeros((128 - rows, 384), F32)], axis=0)
        return total.T

    total = received(2)
    for lv in (2, 1, 0):
        grad_k = unit_back(uc[lv, 192:384, :], total[0:192]) * 0.5
        grad_v = total[192:384] * ROOT_HALF
        if lv > 0:
            base = received(lv - 1)
        else:
            base = down[...]
            for j in range(2):
                arrived(ret0.at[j], br_sem.at[9 + j], bs_sem.at[9 + j])
                base += ret0[j].astype(F32)
            base = round_low(base).T
        total = base + jnp.concatenate([spread(grad_k, lv), spread(grad_v, lv)], axis=0)
    dkv = jnp.concatenate([unit_back(u0[192:384, :], total[0:192]), total[192:384]], axis=0)
    dkvt[...] = dkv.astype(BF16)
    remote(dkvt, pdkvt, cs_sem.at[3], cr_sem.at[3], {"seq": peer}).start()

    def emit_tokens(j, total):
        gts[j] = own_columns(j, total + gtacc[j])

    column_parts(nt(permt[...], dkvt[...]).astype(BF16), wqkv_ref.at[pl.ds(192, 384)], emit_tokens)
    for k in range(1, 4):
        remote(
            gts.at[mp_dev(k)], gtr.at[k - 1], ms_sem.at[2 + k], mr_sem.at[2 + k],
            {"mp": mp_dev(k)},
        ).start()
    z_stage(0)
    first = nt(tg[core, :, 0:256], dkvt[...])
    arrived(pdkvt, cr_sem.at[3], cs_sem.at[3])
    y_stage(1, first + nt(ptg[:, 0:256], pdkvt[...]))

    def mp_finish(sent, got, base, out):
        total = sent[m].astype(F32)
        for k in range(3):
            arrived(got.at[k], mr_sem.at[base + k], ms_sem.at[base + k])
            total += got[k].astype(F32)
        out[...] = total.astype(BF16)

    mp_finish(mixs, mixr, 0, mixed_ref)
    z_stage(1)
    mp_finish(gts, gtr, 3, gt_ref)
    z_finish(0, oa_ref)
    z_finish(1, ob_ref)

    for i in range(9):
        left(dsendc.at[i], fs_sem.at[i], fr_sem.at[i])
        left(dsendc.at[i], bs_sem.at[i], br_sem.at[i])
    for i in range(2):
        left(dsend0.at[i], fs_sem.at[9 + i], fr_sem.at[9 + i])
        left(dsend0.at[i], bs_sem.at[9 + i], br_sem.at[9 + i])
    left(ptg, cs_sem.at[0], cr_sem.at[0])
    left(ra.at[pl.ds(192, 192), pl.ds(256, 256)], cs_sem.at[1], cr_sem.at[1])
    left(ra.at[pl.ds(0, 192), pl.ds(0, 256)], cs_sem.at[2], cr_sem.at[2])
    left(dkvt, cs_sem.at[3], cr_sem.at[3])
    for i in range(6):
        left(mixs.at[0], ms_sem.at[i], mr_sem.at[i])
        left(gs.at[0, pl.ds(0, 96)], ys_sem.at[i], yr_sem.at[i])
    for i in range(14):
        left(zs.at[0, pl.ds(0, 16)], zs_sem.at[i], zr_sem.at[i])


def shards(tokens, w_qkv, w_out, grad_y):
    vmem = pl.BlockSpec(memory_space=pltpu.VMEM)
    low = lambda *shape: pltpu.VMEM(shape, BF16)
    wide = lambda *shape: pltpu.VMEM(shape, F32)
    sems = lambda count: pltpu.SemaphoreType.DMA((count,))
    scratch = [
        low(256, 256), wide(576, 256), wide(3, 384, 128),
        low(3, 256, 384), low(9, 128, 384), low(3, 128, 384), low(3, 384, 256), low(9, 384, 128),
        low(3, 256, 768), low(9, 128, 384), low(256, 768), low(3, 256, 384),
        low(256, 768), low(3, 256, 384), wide(8, 768), wide(3, 8, 384),
        wide(192, 256), wide(192, 128), wide(8, 768), wide(8, 384), low(192, 256), low(192, 256),
        wide(192, 256), wide(3, 192, 128), wide(256, 384),
        low(2, 256, 384), low(9, 128, 384), low(2, 256, 384), low(9, 128, 384),
        low(2, 384, 512), low(384, 512), low(384, 512), low(384, 512), low(384, 256), low(384, 256),
        low(4, 256, 192), low(3, 256, 192), wide(4, 256, 256), low(4, 256, 192), low(3, 256, 192),
        wide(2, 384, 384), low(2, 384, 384), low(2, 3, 96, 384), low(2, 128, 384),
        low(2, 7, 16, 384),
        sems(11), sems(11), sems(11), sems(11), sems(4), sems(4),
        sems(6), sems(6), sems(6), sems(6), sems(14), sems(14),
    ]
    mixed, grad_tokens, part_a, part_b = pl.pallas_call(
        kernel,
        out_shape=(
            jax.ShapeDtypeStruct((256, 192), BF16),
            jax.ShapeDtypeStruct((256, 192), BF16),
            jax.ShapeDtypeStruct((16, 384), F32),
            jax.ShapeDtypeStruct((16, 384), F32),
        ),
        in_specs=[vmem] * 4,
        out_specs=(vmem,) * 4,
        scratch_shapes=scratch,
        compiler_params=pltpu.CompilerParams(
            collective_id=0, has_side_effects=True, vmem_limit_bytes=48 * 1024 * 1024
        ),
        cost_estimate=pl.CostEstimate(
            flops=2_000_000_000, bytes_accessed=4_000_000, transcendentals=1_000_000
        ),
    )(
        tokens.reshape(256, 768), w_qkv.reshape(576, 768), w_out, grad_y.reshape(256, 768)
    )
    grad_wqkv = jnp.stack([part_a[:12, :192], part_b[:12, :192], part_b[:12, 192:]], axis=1)
    grad_wout = part_a[:12, 192:]
    return (mixed[None], grad_tokens[None], grad_wqkv, grad_wout)


def solution(mesh):
    in_specs = (P(None, "seq", None), P(None, "mp", None), P("mp", None), P(None, "seq", None))
    out_specs = (P(None, "seq", "mp"), P(None, "seq", "mp"), P("seq", None, "mp"), P("seq", "mp"))
    return jax.shard_map(shards, mesh=mesh, in_specs=in_specs, out_specs=out_specs, check_vma=False)
```

```python
import jax
import jax.numpy as jnp
from jax import lax
from jax.experimental import pallas as pl
from jax.experimental.pallas import tpu as pltpu
from jax.sharding import PartitionSpec as P

F32 = jnp.float32
BF16 = jnp.bfloat16
MESH = pl.DeviceIdType.MESH
EPS = 1e-06
ROOT_HALF = 0.7071067811865476
NORM = 1.0 / 128.0


def nn(a, b):
    return jnp.dot(a, b, preferred_element_type=F32)


def nt(a, b):
    return lax.dot_general(a, b, (((1,), (1,)), ((), ())), preferred_element_type=F32)


def unit_parts(x):
    heads = x.reshape(x.shape[0] // 64, 64, x.shape[1])
    scale = lax.rsqrt(jnp.mean(heads * heads, axis=1, keepdims=True) + EPS)
    return heads * scale, scale


def unit(x):
    return unit_parts(x)[0].reshape(x.shape)


def unit_back(x, grad):
    y, scale = unit_parts(x)
    dy = grad.reshape(y.shape)
    return (scale * (dy - y * jnp.mean(y * dy, axis=1, keepdims=True))).reshape(x.shape)


def round_low(x):
    return x.astype(BF16).astype(F32)


def iota(shape, dim):
    return lax.broadcasted_iota(jnp.int32, shape, dim)


def one_hot(cond):
    return jnp.where(cond, 1.0, 0.0).astype(BF16)


def natural_token(row):
    high = row >> 5
    return (row & 31) * 8 + (((high & 1) << 2) | (high & 2) | ((high >> 2) & 1))


def kernel(
    tok_hbm, wqkv_hbm, wout_hbm, gy_hbm,
    mixed_ref, gt_ref, gw_ref, go_ref,
    tok_ref, wqkv_ref, wout_ref, gy_ref, wot, wqt, wkvt,
    perm_s, u0, uc, kv0, kvc, ownc, kvt0, kvtc, w0, wc, qm0, qmc, gm0, gmc, c0, cc,
    num0, numc, den0, denc, dot_s, att_s, dq0, dqc, down, dsend0, dsendc, ret0, ret1, retc,
    own1, ownf, sib1, sibc, out1, outc,
    tg, ptg, ra, pra, dkvt, pdkvt, mixs, mixr, gtacc, gts, gtr,
    gf, gs, yr, zs, zr,
    in_sem, fs_sem, fr_sem, hs_sem, hr_sem, bs_sem, br_sem, ss_sem, sr_sem,
    cs_sem, cr_sem, ms_sem, mr_sem, ys_sem, yr_sem, zs_sem, zr_sem,
):
    loads = [
        pltpu.make_async_copy(src, dst, in_sem.at[n])
        for n, (src, dst) in enumerate((
            (tok_hbm, tok_ref),
            (wqkv_hbm.at[pl.ds(192, 384)], wqkv_ref.at[pl.ds(192, 384)]),
            (wqkv_hbm.at[pl.ds(0, 192)], wqkv_ref.at[pl.ds(0, 192)]),
            (gy_hbm, gy_ref),
            (wout_hbm, wout_ref),
        ))
    ]
    for load in loads:
        load.start()

    s = lax.axis_index("seq")
    m = lax.axis_index("mp")
    core = lax.rem(s, 2)
    y = lax.rem(s // 2, 4)
    z = s // 8
    position = (s, s // 2, s // 4)
    extent = (64, 32, 16)
    skip = [3 - 6 * lax.rem(position[lv], 2) for lv in range(3)]

    def offset(lv, j):
        return (-2, 2, skip[lv])[j]

    def target(lv, j, part):
        block = lax.rem(position[lv] + offset(lv, j) + extent[lv], extent[lv])
        return block if lv == 0 else block * (1 << lv) + 2 * part + core

    def parts(lv):
        return 2 if lv == 2 else 1

    def back_slot(j):
        return (1, 0, 2)[j]

    prev_dev = lax.rem(s + 63, 64)
    next_dev = lax.rem(s + 1, 64)
    peer = s + 1 - 2 * core

    def y_dev(k):
        return z * 8 + lax.rem(y + k, 4) * 2 + core

    def z_dev(k):
        return lax.rem(z + k, 8) * 8 + y * 2 + core

    def mp_dev(k):
        return lax.rem(m + k, 4)

    barrier = pltpu.get_barrier_semaphore()
    partners = [{"seq": prev_dev}, {"seq": next_dev}]
    for lv in range(3):
        for j in range(2 if lv == 0 else 3):
            for part in range(parts(lv)):
                partners.append({"seq": target(lv, j, part)})
    partners += [{"seq": y_dev(k)} for k in range(1, 4)]
    partners += [{"seq": z_dev(k)} for k in range(1, 8)]
    partners += [{"mp": mp_dev(k)} for k in range(1, 4)]
    for partner in partners:
        pl.semaphore_signal(barrier, inc=1, device_id=partner, device_id_type=MESH)

    def remote(src, dst, send, recv, where):
        return pltpu.make_async_remote_copy(
            src_ref=src, dst_ref=dst, send_sem=send, recv_sem=recv,
            device_id=where, device_id_type=MESH,
        )

    def arrived(ref, sem, spare):
        remote(ref, ref, spare, sem, {"seq": peer}).wait_recv()

    def left(ref, sem, spare):
        remote(ref, ref, sem, spare, {"seq": peer}).wait_send()

    perm = one_hot(natural_token(iota((256, 256), 0)) == iota((256, 256), 1))
    perm_s[...] = perm
    loads[0].wait()
    tok_p = nn(perm, tok_ref[...]).astype(BF16)
    loads[1].wait()
    u0[192:576, :] = nt(wqkv_ref[192:576, :], tok_p)

    def halves(x, lv):
        return x[:, 0:128] + x[:, 128:256] if lv == 0 else x + pltpu.roll(x, 128 >> lv, 1)

    key = unit(u0[192:384, :])
    v = u0[384:576, :]
    kv0[1] = jnp.concatenate([key, v], axis=0).T.astype(BF16)
    for lv in range(3):
        mean = halves(key, lv) * 0.5
        v = halves(v, lv) * ROOT_HALF
        uc[lv, 192:384, :] = mean
        key = unit(mean)
        ownc[lv] = jnp.concatenate([key, v], axis=0).T.astype(BF16)

    pl.semaphore_wait(barrier, len(partners))

    mine = (0, core * 64, core * 64 + lax.rem(s // 2, 2) * 32)
    for lv in range(3):
        rows = 128 >> lv
        for j in range(2 if lv == 0 else 3):
            i = 3 * lv + back_slot(j)
            for part in range(parts(lv)):
                remote(
                    ownc.at[lv, pl.ds(0, rows)],
                    kvc.at[i, pl.ds(mine[lv], rows)],
                    fs_sem.at[i], fr_sem.at[i], {"seq": target(lv, j, part)},
                ).start()
    remote(kv0.at[1], kv0.at[0], fs_sem.at[9], fr_sem.at[9], {"seq": next_dev}).start()
    remote(kv0.at[1], kv0.at[2], fs_sem.at[10], fr_sem.at[10], {"seq": prev_dev}).start()

    def store_q(dst, q_rows, n):
        dst[...] = jnp.zeros(dst.shape, BF16)
        half = (q_rows * 0.5).astype(BF16)
        for h in range(3):
            dst[64 * h : 64 * h + 64, h * n : h * n + n] = half[64 * h : 64 * h + 64]

    loads[2].wait()
    u0[0:192, :] = nt(wqkv_ref[0:192, :], tok_p)
    query = unit(u0[0:192, :])
    store_q(qm0, query, 256)
    for lv in range(3):
        mean = halves(query, lv) * 0.5
        uc[lv, 0:192, :] = mean
        query = unit(mean)
        store_q(qmc.at[lv], query, 128)

    num0[...] = jnp.zeros(num0.shape, F32)
    numc[...] = jnp.zeros(numc.shape, F32)
    den0[...] = jnp.zeros(den0.shape, F32)
    denc[...] = jnp.zeros(denc.shape, F32)
    dq0[...] = jnp.zeros(dq0.shape, F32)
    dqc[...] = jnp.zeros(dqc.shape, F32)
    ra[...] = jnp.zeros(ra.shape, BF16)
    pra[0:192, 256:512] = jnp.zeros((192, 256), BF16)
    pra[192:384, 0:256] = jnp.zeros((192, 256), BF16)

    def forward(keys, keyst, qm, w_ref, num, den, factor, n):
        block = keys[...]
        count = block.shape[0]
        keyst[...] = block.astype(F32).T.astype(BF16)
        for h in range(3):
            lanes = slice(h * n, h * n + n)
            w = jnp.exp(nn(block[:, 0:256], qm[:, lanes])) * factor
            den[:, lanes] += jnp.sum(w.reshape(count // 8, 8, n), axis=0)
            wb = w.astype(BF16)
            w_ref[:, lanes] = wb
            num[64 * h : 64 * h + 64, :] += nn(keyst[192 + 64 * h : 256 + 64 * h, :], wb)

    def keep0(j):
        if j == 1:
            return jnp.float32(1.0)
        inside = s > 0 if j == 0 else s < 63
        return jnp.where(inside, jnp.float32(1.0), jnp.float32(0.0))

    forward(kv0.at[1], kvt0.at[1], qm0, w0.at[1], num0, den0, keep0(1), 256)

    loads[3].wait()
    loads[4].wait()
    gy_p = nn(perm, gy_ref[...]).astype(BF16)
    dot_s[...] = nt(wout_ref[...], gy_p).astype(BF16)
    for half in range(2):
        index = iota((384, 768), 0)
        twelfth = (index * 5462) >> 16
        feature = (twelfth & 7) * 96 + (twelfth >> 3) * 24 + half * 12 + (index - 12 * twelfth)
        pick = one_hot(feature == iota((384, 768), 1))
        tg[half, :, 0:256] = nt(pick, tok_p).astype(BF16)
        tg[half, :, 256:512] = nt(pick, gy_p).astype(BF16)
    remote(tg.at[1 - core], ptg, cs_sem.at[0], cr_sem.at[0], {"seq": peer}).start()

    same = one_hot(iota((256, 256), 0) == iota((256, 256), 1))
    for n in range(3):
        cut = slice(256 * n, 256 * n + 256)
        wot[cut, :] = nt(same, wout_ref[:, cut]).astype(BF16)
        wqt[cut, :] = nt(same, wqkv_ref[0:192, cut]).astype(BF16)
        wkvt[cut, :] = nt(same, wqkv_ref[192:576, cut]).astype(BF16)

    half = core * 64
    other = 64 - half
    arrived(kvc.at[0], fr_sem.at[0], fs_sem.at[0])
    arrived(kvc.at[1], fr_sem.at[1], fs_sem.at[1])
    remote(kvc.at[core], kvc.at[2], hs_sem.at[2], hr_sem.at[2], {"seq": peer}).start()
    for i in range(3, 9):
        piece = kvc.at[i, pl.ds(half, 64)]
        arrived(piece, fr_sem.at[i], fs_sem.at[i])
        remote(piece, piece, hs_sem.at[i], hr_sem.at[i], {"seq": peer}).start()

    def coarse_forward(lv, j):
        i = 3 * lv + j
        place = position[lv] + offset(lv, j)
        inside = (place >= 0) & (place < extent[lv])
        factor = jnp.where(inside, jnp.float32(2 << lv), jnp.float32(0.0))
        forward(kvc.at[i], kvtc.at[i], qmc.at[lv], wc.at[i], numc, denc, factor, 128)

    coarse_forward(0, 0)
    coarse_forward(0, 1)
    for j in (0, 2):
        arrived(kv0.at[j], fr_sem.at[9 + j // 2], fs_sem.at[9 + j // 2])
        forward(kv0.at[j], kvt0.at[j], qm0, w0.at[j], num0, den0, keep0(j), 256)
    arrived(kvc.at[2], hr_sem.at[2], hs_sem.at[2])
    coarse_forward(0, 2)
    for i in range(3, 9):
        arrived(kvc.at[i, pl.ds(other, 64)], hr_sem.at[i], hs_sem.at[i])
        coarse_forward(i // 3, i % 3)

    lane = iota((1, 128), 1)
    gm0[...] = jnp.zeros(gm0.shape, BF16)
    gmc[...] = jnp.zeros(gmc.shape, BF16)
    for h in range(3):
        rows = slice(64 * h, 64 * h + 64)
        grows = slice(64 * h + 64, 64 * h + 128)
        coarse = jnp.sum(denc[:, 128 * h : 128 * h + 128], axis=0, keepdims=True)
        den = jnp.sum(den0[:, 256 * h : 256 * h + 256], axis=0, keepdims=True)
        inverse = 1.0 / (den + jnp.concatenate([coarse, coarse], axis=1))
        more = numc[rows, :]
        att = ((num0[rows, :] + jnp.concatenate([more, more], axis=1)) * inverse).astype(BF16)
        ra[192 + 64 * h : 256 + 64 * h, 256:512] = att
        att_s[rows, :] = att
        d_att = dot_s[rows, :].astype(F32)
        g = d_att * inverse
        c = jnp.sum(d_att * att.astype(F32), axis=0, keepdims=True) * inverse
        gm0[grows, 256 * h : 256 * h + 256] = g.astype(BF16)
        c0[:, 256 * h : 256 * h + 256] = jnp.broadcast_to(c, (8, 256))
        g = g[:, 0:128] + g[:, 128:256]
        c = c[:, 0:128] + c[:, 128:256]
        for lv in range(3):
            if lv > 0:
                g = g + pltpu.roll(g, 128 >> lv, 1)
                c = c + pltpu.roll(jnp.broadcast_to(c, (8, 128)), 128 >> lv, 1)[0:1]
            used = lane < (128 >> lv)
            gmc[lv, grows, 128 * h : 128 * h + 128] = jnp.where(used, g, 0.0).astype(BF16)
            cc[lv, :, 128 * h : 128 * h + 128] = jnp.broadcast_to(
                jnp.where(used, c, 0.0), (8, 128)
            )
    remote(
        ra.at[pl.ds(192, 192), pl.ds(256, 256)], pra.at[pl.ds(192, 192), pl.ds(256, 256)],
        cs_sem.at[1], cr_sem.at[1], {"seq": peer},
    ).start()

    def backward(keys, keyst, qm, gm, c_rows, w_ref, dq, n):
        count = keys.shape[0]
        dk = jnp.zeros((count, 256), F32)
        dv = jnp.zeros((count, 256), F32)
        for h in range(3):
            lanes = slice(h * n, h * n + n)
            wb = w_ref[:, lanes]
            inner = nn(keys[:, 128:384], gm[:, lanes])
            slope = (wb.astype(F32) * (inner - c_rows[0:1, lanes])).astype(BF16)
            dq[64 * h : 64 * h + 64, :] += nn(keyst[64 * h : 64 * h + 64, :], slope)
            dk += nt(slope, qm[:, lanes])
            dv += nt(wb, gm[:, lanes])
        return jnp.concatenate(
            [dk[:, 0:128], dk[:, 128:256] + dv[:, 0:128], dv[:, 128:256]], axis=1
        )

    def coarse_backward(lv, i):
        return backward(
            kvc.at[i], kvtc.at[i], qmc.at[lv], gmc.at[lv], cc.at[lv], wc.at[i], dqc.at[lv], 128
        )

    def to_peer(i):
        ownf[i - 3] = coarse_backward(i // 3, i)
        dsendc[i - 3] = ownf[i - 3, pl.ds(other, 64), :].astype(BF16)
        remote(
            dsendc.at[i - 3], sibc.at[i - 3], ss_sem.at[i], sr_sem.at[i], {"seq": peer}
        ).start()

    def return_pair(i):
        lv, j = i // 3, i % 3
        arrived(sibc.at[i - 3], sr_sem.at[i], ss_sem.at[i])
        outc[i - 3] = (
            ownf[i - 3, pl.ds(half, 64), :] + sibc[i - 3].astype(F32)
        ).astype(BF16)
        k = 3 * lv + back_slot(j)
        rows = 128 >> lv
        into = 0 if lv == 1 else lax.rem(s // 2, 2) * 32
        for part in range(parts(lv)):
            remote(
                outc.at[i - 3, pl.ds(part * rows, rows)], retc.at[k - 3, pl.ds(into, rows)],
                bs_sem.at[k], br_sem.at[k], {"seq": target(lv, j, part)},
            ).start()

    def return_first(slot, value):
        out1[slot] = value.astype(BF16)
        where = lax.rem(s + 4 * slot - 2 + 64, 64)
        remote(
            out1.at[slot], ret1.at[1 - slot], bs_sem.at[1 - slot], br_sem.at[1 - slot],
            {"seq": where},
        ).start()

    def near_backward(j):
        dsend0[j // 2] = backward(
            kv0.at[j], kvt0.at[j], qm0, gm0, c0, w0.at[j], dq0, 256
        ).astype(BF16)
        k = 1 - j // 2
        remote(
            dsend0.at[j // 2], ret0.at[k], bs_sem.at[9 + k], br_sem.at[9 + k],
            {"seq": prev_dev if j == 0 else next_dev},
        ).start()

    for i in range(6, 9):
        to_peer(i)
    for i in range(3, 6):
        to_peer(i)
    own1[...] = coarse_backward(0, 2).astype(BF16)
    remote(own1, sib1, ss_sem.at[2], sr_sem.at[2], {"seq": peer}).start()
    return_first(1 - core, coarse_backward(0, 1 - core))
    for i in range(6, 9):
        return_pair(i)
    shared = coarse_backward(0, core)
    for i in range(3, 6):
        return_pair(i)
    arrived(sib1, sr_sem.at[2], ss_sem.at[2])
    return_first(core, shared + sib1[...].astype(F32))
    near_backward(0)
    near_backward(2)
    down[...] = backward(kv0.at[1], kvt0.at[1], qm0, gm0, c0, w0.at[1], dq0, 256)

    def spread(grad, lv):
        if lv == 0:
            return jnp.concatenate([grad, grad], axis=1)
        return grad + pltpu.roll(grad, 128 >> lv, 1)

    grad = round_low(dqc[2] * 0.5)
    for lv in (2, 1, 0):
        grad = unit_back(uc[lv, 0:192, :], grad) * 0.5
        base = dqc[lv - 1] if lv > 0 else dq0[...]
        grad = round_low(base * 0.5) + spread(grad, lv)
    dq_t = unit_back(u0[0:192, :], grad).astype(BF16)
    ra[0:192, 0:256] = dq_t
    remote(
        ra.at[pl.ds(0, 192), pl.ds(0, 256)], pra.at[pl.ds(0, 192), pl.ds(0, 256)],
        cs_sem.at[2], cr_sem.at[2], {"seq": peer},
    ).start()

    att_t = att_s[...]
    for j in range(4):
        mixs[j] = nn(wot[192 * j : 192 * j + 192, :], att_t).astype(BF16)
    for k in range(1, 4):
        remote(
            mixs.at[mp_dev(k)], mixr.at[k - 1], ms_sem.at[k - 1], mr_sem.at[k - 1],
            {"mp": mp_dev(k)},
        ).start()
    for j in range(4):
        gtacc[j] = nn(wqt[192 * j : 192 * j + 192, :], dq_t)

    def y_stage(r, total):
        gf[r] = total
        gs[r] = total.astype(BF16)
        for k in range(1, 4):
            remote(
                gs.at[r, pl.ds(lax.rem(y + k, 4) * 96, 96)], yr.at[r, k - 1],
                ys_sem.at[3 * r + k - 1], yr_sem.at[3 * r + k - 1], {"seq": y_dev(k)},
            ).start()

    at16 = iota((128, 96), 0)
    widen = one_hot(
        ((at16 >> 4) * 12 + (at16 & 15) == iota((128, 96), 1)) & ((at16 & 15) < 12)
    )

    def z_stage(r):
        total = gf[r, pl.ds(y * 96, 96), :]
        for k in range(3):
            arrived(yr.at[r, k], yr_sem.at[3 * r + k], ys_sem.at[3 * r + k])
            total += yr[r, k].astype(F32)
        zs[r] = nn(widen, total.astype(BF16)).astype(BF16)
        for k in range(1, 8):
            remote(
                zs.at[r, pl.ds(lax.rem(z + k, 8) * 16, 16)], zr.at[r, k - 1],
                zs_sem.at[7 * r + k - 1], zr_sem.at[7 * r + k - 1], {"seq": z_dev(k)},
            ).start()

    def z_finish(r):
        total = zs[r, pl.ds(z * 16, 16), :].astype(F32)
        for k in range(7):
            arrived(zr.at[r, k], zr_sem.at[7 * r + k], zs_sem.at[7 * r + k])
            total += zr[r, k].astype(F32)
        return total * NORM

    arrived(ptg, cr_sem.at[0], cs_sem.at[0])
    arrived(pra.at[pl.ds(192, 192), pl.ds(256, 256)], cr_sem.at[1], cs_sem.at[1])
    arrived(pra.at[pl.ds(0, 192), pl.ds(0, 256)], cr_sem.at[2], cs_sem.at[2])
    y_stage(0, nt(tg[core], ra[...]) + nt(ptg[...], pra[...]))

    def received(lv):
        if lv == 0:
            total = jnp.zeros((128, 384), F32)
            for i in range(2):
                arrived(ret1.at[i], br_sem.at[i], bs_sem.at[i])
                total += ret1[i].astype(F32)
        else:
            total = jnp.zeros((64, 384), F32)
            for i in range(3 * lv, 3 * lv + 3):
                arrived(retc.at[i - 3], br_sem.at[i], bs_sem.at[i])
                total += retc[i - 3].astype(F32)
            if lv == 2:
                total = total[0:32] + total[32:64]
        total = round_low(total)
        if lv > 0:
            rows = 128 >> lv
            total = jnp.concatenate([total, jnp.zeros((128 - rows, 384), F32)], axis=0)
        return total.T

    total = received(2)
    for lv in (2, 1, 0):
        grad_k = unit_back(uc[lv, 192:384, :], total[0:192]) * 0.5
        grad_v = total[192:384] * ROOT_HALF
        if lv > 0:
            base = received(lv - 1)
        else:
            base = down[...]
            for j in range(2):
                arrived(ret0.at[j], br_sem.at[9 + j], bs_sem.at[9 + j])
                base += ret0[j].astype(F32)
            base = round_low(base).T
        total = base + jnp.concatenate([spread(grad_k, lv), spread(grad_v, lv)], axis=0)
    dkv = jnp.concatenate([unit_back(u0[192:384, :], total[0:192]), total[192:384]], axis=0)
    dkvt[...] = dkv.astype(BF16)
    remote(dkvt, pdkvt, cs_sem.at[3], cr_sem.at[3], {"seq": peer}).start()

    dkv_t = dkvt[...]
    for j in range(4):
        gts[j] = (nn(wkvt[192 * j : 192 * j + 192, :], dkv_t) + gtacc[j]).astype(BF16)
    for k in range(1, 4):
        remote(
            gts.at[mp_dev(k)], gtr.at[k - 1], ms_sem.at[2 + k], mr_sem.at[2 + k],
            {"mp": mp_dev(k)},
        ).start()
    z_stage(0)
    first = nt(tg[core, :, 0:256], dkvt[...])
    arrived(pdkvt, cr_sem.at[3], cs_sem.at[3])
    y_stage(1, first + nt(ptg[:, 0:256], pdkvt[...]))

    def mp_finish(sent, got, base, out):
        total = sent[m].astype(F32)
        for k in range(3):
            arrived(got.at[k], mr_sem.at[base + k], ms_sem.at[base + k])
            total += got[k].astype(F32)
        out[...] = nn(total.astype(BF16), perm_s[...]).astype(BF16)

    mp_finish(mixs, mixr, 0, mixed_ref)
    z_stage(1)
    mp_finish(gts, gtr, 3, gt_ref)
    first = z_finish(0)
    go_ref[...] = pltpu.roll(first, 192, 1)[0:12, 0:192]
    gw_ref[:, 0, :] = first[0:12, 0:192]
    second = z_finish(1)
    gw_ref[:, 1, :] = second[0:12, 0:192]
    gw_ref[:, 2, :] = pltpu.roll(second, 192, 1)[0:12, 0:192]

    for i in range(2):
        left(out1.at[i], fs_sem.at[i], fr_sem.at[i])
        left(out1.at[i], bs_sem.at[i], br_sem.at[i])
        left(dsend0.at[i], fs_sem.at[9 + i], fr_sem.at[9 + i])
        left(dsend0.at[i], bs_sem.at[9 + i], br_sem.at[9 + i])
    left(own1, hs_sem.at[2], hr_sem.at[2])
    left(own1, ss_sem.at[2], sr_sem.at[2])
    for i in range(3, 9):
        left(outc.at[i - 3], fs_sem.at[i], fr_sem.at[i])
        left(outc.at[i - 3], hs_sem.at[i], hr_sem.at[i])
        left(outc.at[i - 3], ss_sem.at[i], sr_sem.at[i])
        left(outc.at[i - 3], bs_sem.at[i], br_sem.at[i])
    left(ptg, cs_sem.at[0], cr_sem.at[0])
    left(ra.at[pl.ds(192, 192), pl.ds(256, 256)], cs_sem.at[1], cr_sem.at[1])
    left(ra.at[pl.ds(0, 192), pl.ds(0, 256)], cs_sem.at[2], cr_sem.at[2])
    left(dkvt, cs_sem.at[3], cr_sem.at[3])
    for i in range(6):
        left(mixs.at[0], ms_sem.at[i], mr_sem.at[i])
        left(gs.at[0, pl.ds(0, 96)], ys_sem.at[i], yr_sem.at[i])
    for i in range(14):
        left(zs.at[0, pl.ds(0, 16)], zs_sem.at[i], zr_sem.at[i])


def deliver(*refs):
    count = (len(refs) - 1) // 2
    copies = [
        pltpu.make_async_copy(refs[n], refs[count + n], refs[-1].at[n]) for n in range(count)
    ]
    for copy in copies:
        copy.start()
    for copy in copies:
        copy.wait()


def shards(tokens, w_qkv, w_out, grad_y):
    vmem = pl.BlockSpec(memory_space=pltpu.VMEM)
    hbm = pl.BlockSpec(memory_space=pltpu.HBM)
    low = lambda *shape: pltpu.VMEM(shape, BF16)
    wide = lambda *shape: pltpu.VMEM(shape, F32)
    sems = lambda count: pltpu.SemaphoreType.DMA((count,))
    scratch = [
        low(256, 768), low(576, 768), low(192, 768), low(256, 768),
        low(768, 192), low(768, 192), low(768, 384),
        low(256, 256), wide(576, 256), wide(3, 384, 128),
        low(3, 256, 384), low(9, 128, 384), low(3, 128, 384), low(3, 384, 256), low(9, 384, 128),
        low(3, 256, 768), low(9, 128, 384), low(256, 768), low(3, 256, 384),
        low(256, 768), low(3, 256, 384), wide(8, 768), wide(3, 8, 384),
        wide(192, 256), wide(192, 128), wide(8, 768), wide(8, 384), low(192, 256), low(192, 256),
        wide(192, 256), wide(3, 192, 128), wide(256, 384),
        low(2, 256, 384), low(6, 64, 384), low(2, 256, 384), low(2, 128, 384), low(6, 64, 384),
        low(128, 384), wide(6, 128, 384), low(128, 384), low(6, 64, 384),
        low(2, 128, 384), low(6, 64, 384),
        low(2, 384, 512), low(384, 512), low(384, 512), low(384, 512), low(384, 256), low(384, 256),
        low(4, 192, 256), low(3, 192, 256), wide(4, 192, 256), low(4, 192, 256), low(3, 192, 256),
        wide(2, 384, 384), low(2, 384, 384), low(2, 3, 96, 384), low(2, 128, 384),
        low(2, 7, 16, 384),
        sems(5), sems(11), sems(11), sems(9), sems(9), sems(11), sems(11), sems(9), sems(9),
        sems(4), sems(4), sems(6), sems(6), sems(6), sems(6), sems(14), sems(14),
    ]
    shapes = (
        jax.ShapeDtypeStruct((192, 256), BF16),
        jax.ShapeDtypeStruct((192, 256), BF16),
        jax.ShapeDtypeStruct((12, 3, 192), F32),
        jax.ShapeDtypeStruct((12, 192), F32),
    )
    results = pl.pallas_call(
        kernel,
        out_shape=shapes,
        in_specs=[hbm] * 4,
        out_specs=(vmem,) * 4,
        scratch_shapes=scratch,
        compiler_params=pltpu.CompilerParams(
            collective_id=0, has_side_effects=True, vmem_limit_bytes=56098816
        ),
        cost_estimate=pl.CostEstimate(
            flops=2_000_000_000, bytes_accessed=4_000_000, transcendentals=1_000_000
        ),
    )(
        tokens.reshape(256, 768), w_qkv.reshape(576, 768), w_out, grad_y.reshape(256, 768)
    )
    mixed, grad_tokens, grad_wqkv, grad_wout = pl.pallas_call(
        deliver,
        out_shape=shapes,
        in_specs=[vmem] * 4,
        out_specs=(hbm,) * 4,
        scratch_shapes=[sems(4)],
    )(*results)
    return (mixed.T[None], grad_tokens.T[None], grad_wqkv, grad_wout)


def solution(mesh):
    in_specs = (P(None, "seq", None), P(None, "mp", None), P("mp", None), P(None, "seq", None))
    out_specs = (P(None, "seq", "mp"), P(None, "seq", "mp"), P("seq", None, "mp"), P("seq", "mp"))
    return jax.shard_map(shards, mesh=mesh, in_specs=in_specs, out_specs=out_specs, check_vma=False)
```

```python
import jax
import jax.numpy as jnp
from jax import lax
from jax.experimental import pallas as pl
from jax.experimental.pallas import tpu as pltpu
from jax.sharding import PartitionSpec as P

F32 = jnp.float32
BF16 = jnp.bfloat16
MESH = pl.DeviceIdType.MESH
EPS = 1e-06
ROOT_HALF = 0.7071067811865476
NORM = 1.0 / 128.0


def nn(a, b):
    return jnp.dot(a, b, preferred_element_type=F32)


def nt(a, b):
    return lax.dot_general(a, b, (((1,), (1,)), ((), ())), preferred_element_type=F32)


def unit_parts(x):
    heads = x.reshape(x.shape[0] // 64, 64, x.shape[1])
    scale = lax.rsqrt(jnp.mean(heads * heads, axis=1, keepdims=True) + EPS)
    return heads * scale, scale


def unit(x):
    return unit_parts(x)[0].reshape(x.shape)


def unit_back(x, grad):
    y, scale = unit_parts(x)
    dy = grad.reshape(y.shape)
    return (scale * (dy - y * jnp.mean(y * dy, axis=1, keepdims=True))).reshape(x.shape)


def round_low(x):
    return x.astype(BF16).astype(F32)


def iota(shape, dim):
    return lax.broadcasted_iota(jnp.int32, shape, dim)


def one_hot(cond):
    return jnp.where(cond, 1.0, 0.0).astype(BF16)


def natural_token(row):
    high = row >> 5
    return (row & 31) * 8 + (((high & 1) << 2) | (high & 2) | ((high >> 2) & 1))


def kernel(
    tok_hbm, wqkv_hbm, wout_hbm, gy_hbm,
    mixed_ref, gt_ref, gw_ref, go_ref,
    tok_ref, wqkv_ref, wout_ref, gy_ref, wot, wqt, wkvt,
    perm_s, u0, uc, kv0, kvc, ownc, kvt0, kvtc, w0, wc, qm0, qmc, gm0, gmc, c0, cc,
    num0, numc, den0, denc, dot_s, att_s, dq0, dqc, down, dsend0, dsendc, ret0, ret1, retc,
    own1, ownf, sib1, sibc, out1, outc,
    tg, ptg, ra, pra, dkvt, pdkvt, mixs, mixr, gtacc, gts, gtr,
    gf, gs, zra, yra, yrb, zrb, wsa, wsb,
    in_sem, fs_sem, fr_sem, hs_sem, hr_sem, bs_sem, br_sem, ss_sem, sr_sem,
    cs_sem, cr_sem, ms_sem, mr_sem, ys_sem, yr_sem, zs_sem, zr_sem,
):
    loads = [
        pltpu.make_async_copy(src, dst, in_sem.at[n])
        for n, (src, dst) in enumerate((
            (tok_hbm, tok_ref),
            (wqkv_hbm.at[pl.ds(192, 384)], wqkv_ref.at[pl.ds(192, 384)]),
            (wqkv_hbm.at[pl.ds(0, 192)], wqkv_ref.at[pl.ds(0, 192)]),
            (gy_hbm, gy_ref),
            (wout_hbm, wout_ref),
        ))
    ]
    for load in loads:
        load.start()

    s = lax.axis_index("seq")
    m = lax.axis_index("mp")
    core = lax.rem(s, 2)
    y = lax.rem(s // 2, 4)
    z = s // 8
    position = (s, s // 2, s // 4)
    extent = (64, 32, 16)
    skip = [3 - 6 * lax.rem(position[lv], 2) for lv in range(3)]

    def offset(lv, j):
        return (-2, 2, skip[lv])[j]

    def target(lv, j, part):
        block = lax.rem(position[lv] + offset(lv, j) + extent[lv], extent[lv])
        return block if lv == 0 else block * (1 << lv) + 2 * part + core

    def parts(lv):
        return 2 if lv == 2 else 1

    def back_slot(j):
        return (1, 0, 2)[j]

    prev_dev = lax.rem(s + 63, 64)
    next_dev = lax.rem(s + 1, 64)
    peer = s + 1 - 2 * core
    across = lax.rem(s + 2 * core + 63, 64)

    def y_dev(k):
        return z * 8 + lax.rem(y + k, 4) * 2 + core

    def z_dev(k):
        return lax.rem(z + k, 8) * 8 + y * 2 + core

    def mp_dev(k):
        return lax.rem(m + k, 4)

    barrier = pltpu.get_barrier_semaphore()
    partners = [{"seq": prev_dev}, {"seq": next_dev}]
    for lv in range(3):
        for j in range(2 if lv == 0 else 3):
            for part in range(parts(lv)):
                partners.append({"seq": target(lv, j, part)})
    partners += [{"seq": y_dev(k)} for k in range(1, 4)]
    partners += [{"seq": z_dev(k)} for k in range(1, 8)]
    partners += [{"mp": mp_dev(k)} for k in range(1, 4)]
    for partner in partners:
        pl.semaphore_signal(barrier, inc=1, device_id=partner, device_id_type=MESH)

    def remote(src, dst, send, recv, where):
        return pltpu.make_async_remote_copy(
            src_ref=src, dst_ref=dst, send_sem=send, recv_sem=recv,
            device_id=where, device_id_type=MESH,
        )

    def arrived(ref, sem, spare):
        remote(ref, ref, spare, sem, {"seq": peer}).wait_recv()

    def left(ref, sem, spare):
        remote(ref, ref, sem, spare, {"seq": peer}).wait_send()

    perm = one_hot(natural_token(iota((256, 256), 0)) == iota((256, 256), 1))
    perm_s[...] = perm
    loads[0].wait()
    tok_p = nn(perm, tok_ref[...]).astype(BF16)
    loads[1].wait()
    u0[192:576, :] = nt(wqkv_ref[192:576, :], tok_p)

    def halves(x, lv):
        return x[:, 0:128] + x[:, 128:256] if lv == 0 else x + pltpu.roll(x, 128 >> lv, 1)

    key = unit(u0[192:384, :])
    v = u0[384:576, :]
    kv0[1] = jnp.concatenate([key, v], axis=0).T.astype(BF16)
    for lv in range(3):
        mean = halves(key, lv) * 0.5
        v = halves(v, lv) * ROOT_HALF
        uc[lv, 192:384, :] = mean
        key = unit(mean)
        ownc[lv] = jnp.concatenate([key, v], axis=0).T.astype(BF16)

    pl.semaphore_wait(barrier, len(partners))

    mine = (0, core * 64, core * 64 + lax.rem(s // 2, 2) * 32)
    for lv in (2, 1, 0):
        rows = 128 >> lv
        for j in range(2 if lv == 0 else 3):
            i = 3 * lv + back_slot(j)
            for part in range(parts(lv)):
                remote(
                    ownc.at[lv, pl.ds(0, rows)],
                    kvc.at[i, pl.ds(mine[lv], rows)],
                    fs_sem.at[i], fr_sem.at[i], {"seq": target(lv, j, part)},
                ).start()
    remote(kv0.at[1], kv0.at[2 * core], fs_sem.at[9], fr_sem.at[9], {"seq": peer}).start()
    remote(kv0.at[1], kv0.at[2 - 2 * core], fs_sem.at[10], fr_sem.at[10], {"seq": across}).start()

    def store_q(dst, q_rows, n):
        dst[...] = jnp.zeros(dst.shape, BF16)
        half = (q_rows * 0.5).astype(BF16)
        for h in range(3):
            dst[64 * h : 64 * h + 64, h * n : h * n + n] = half[64 * h : 64 * h + 64]

    loads[2].wait()
    u0[0:192, :] = nt(wqkv_ref[0:192, :], tok_p)
    query = unit(u0[0:192, :])
    store_q(qm0, query, 256)
    for lv in range(3):
        mean = halves(query, lv) * 0.5
        uc[lv, 0:192, :] = mean
        query = unit(mean)
        store_q(qmc.at[lv], query, 128)

    num0[...] = jnp.zeros(num0.shape, F32)
    numc[...] = jnp.zeros(numc.shape, F32)
    den0[...] = jnp.zeros(den0.shape, F32)
    denc[...] = jnp.zeros(denc.shape, F32)
    dq0[...] = jnp.zeros(dq0.shape, F32)
    dqc[...] = jnp.zeros(dqc.shape, F32)
    ra[...] = jnp.zeros(ra.shape, BF16)
    pra[0:192, 256:512] = jnp.zeros((192, 256), BF16)
    pra[192:384, 0:256] = jnp.zeros((192, 256), BF16)

    def forward(keys, keyst, qm, w_ref, num, den, factor, n):
        block = keys[...]
        count = block.shape[0]
        keyst[...] = block.astype(F32).T.astype(BF16)
        for h in range(3):
            lanes = slice(h * n, h * n + n)
            w = jnp.exp(nn(block[:, 0:256], qm[:, lanes])) * factor
            den[:, lanes] += jnp.sum(w.reshape(count // 8, 8, n), axis=0)
            wb = w.astype(BF16)
            w_ref[:, lanes] = wb
            num[64 * h : 64 * h + 64, :] += nn(keyst[192 + 64 * h : 256 + 64 * h, :], wb)

    near, far = 2 - 2 * core, 2 * core
    outside = ((s == 0) & (core == 0)) | ((s == 63) & (core == 1))
    far_keep = jnp.where(outside, jnp.float32(0.0), jnp.float32(1.0))
    one = jnp.float32(1.0)
    forward(kv0.at[1], kvt0.at[1], qm0, w0.at[1], num0, den0, one, 256)

    loads[3].wait()
    loads[4].wait()
    gy_p = nn(perm, gy_ref[...]).astype(BF16)
    dot_s[...] = nt(wout_ref[...], gy_p).astype(BF16)
    for half in range(2):
        index = iota((384, 768), 0)
        twelfth = (index * 5462) >> 16
        rest = half * 12 + (index - 12 * twelfth)
        feature = (twelfth >> 2) * 96 + (twelfth & 3) * 24 + rest
        pick = one_hot(feature == iota((384, 768), 1))
        tg[half, :, 0:256] = nt(pick, tok_p).astype(BF16)
        tg[half, :, 256:512] = nt(pick, gy_p).astype(BF16)
        feature = (twelfth & 7) * 96 + (twelfth >> 3) * 24 + rest
        pick = one_hot(feature == iota((384, 768), 1))
        tg[half, :, 512:768] = nt(pick, tok_p).astype(BF16)
    remote(tg.at[1 - core], ptg, cs_sem.at[0], cr_sem.at[0], {"seq": peer}).start()

    arrived(kv0.at[near], fr_sem.at[9], fs_sem.at[9])
    forward(kv0.at[near], kvt0.at[near], qm0, w0.at[near], num0, den0, one, 256)

    same = one_hot(iota((256, 256), 0) == iota((256, 256), 1))
    for n in range(3):
        cut = slice(256 * n, 256 * n + 256)
        wot[cut, :] = nt(same, wout_ref[:, cut]).astype(BF16)
        wqt[cut, :] = nt(same, wqkv_ref[0:192, cut]).astype(BF16)
        wkvt[cut, :] = nt(same, wqkv_ref[192:576, cut]).astype(BF16)

    half = core * 64
    other = 64 - half
    for i in range(3, 9):
        piece = kvc.at[i, pl.ds(half, 64)]
        arrived(piece, fr_sem.at[i], fs_sem.at[i])
        remote(piece, piece, hs_sem.at[i], hr_sem.at[i], {"seq": peer}).start()
    arrived(kvc.at[0], fr_sem.at[0], fs_sem.at[0])
    arrived(kvc.at[1], fr_sem.at[1], fs_sem.at[1])
    remote(kvc.at[core], kvc.at[2], hs_sem.at[2], hr_sem.at[2], {"seq": peer}).start()

    def coarse_forward(lv, j):
        i = 3 * lv + j
        place = position[lv] + offset(lv, j)
        inside = (place >= 0) & (place < extent[lv])
        factor = jnp.where(inside, jnp.float32(2 << lv), jnp.float32(0.0))
        forward(kvc.at[i], kvtc.at[i], qmc.at[lv], wc.at[i], numc, denc, factor, 128)

    for i in range(3, 9):
        arrived(kvc.at[i, pl.ds(other, 64)], hr_sem.at[i], hs_sem.at[i])
        coarse_forward(i // 3, i % 3)
    coarse_forward(0, 0)
    coarse_forward(0, 1)
    arrived(kvc.at[2], hr_sem.at[2], hs_sem.at[2])
    coarse_forward(0, 2)
    arrived(kv0.at[far], fr_sem.at[10], fs_sem.at[10])
    forward(kv0.at[far], kvt0.at[far], qm0, w0.at[far], num0, den0, far_keep, 256)

    lane = iota((1, 128), 1)
    gm0[...] = jnp.zeros(gm0.shape, BF16)
    gmc[...] = jnp.zeros(gmc.shape, BF16)
    for h in range(3):
        rows = slice(64 * h, 64 * h + 64)
        grows = slice(64 * h + 64, 64 * h + 128)
        coarse = jnp.sum(denc[:, 128 * h : 128 * h + 128], axis=0, keepdims=True)
        den = jnp.sum(den0[:, 256 * h : 256 * h + 256], axis=0, keepdims=True)
        inverse = 1.0 / (den + jnp.concatenate([coarse, coarse], axis=1))
        more = numc[rows, :]
        att = ((num0[rows, :] + jnp.concatenate([more, more], axis=1)) * inverse).astype(BF16)
        ra[192 + 64 * h : 256 + 64 * h, 256:512] = att
        att_s[rows, :] = att
        d_att = dot_s[rows, :].astype(F32)
        g = d_att * inverse
        c = jnp.sum(d_att * att.astype(F32), axis=0, keepdims=True) * inverse
        gm0[grows, 256 * h : 256 * h + 256] = g.astype(BF16)
        c0[:, 256 * h : 256 * h + 256] = jnp.broadcast_to(c, (8, 256))
        g = g[:, 0:128] + g[:, 128:256]
        c = c[:, 0:128] + c[:, 128:256]
        for lv in range(3):
            if lv > 0:
                g = g + pltpu.roll(g, 128 >> lv, 1)
                c = c + pltpu.roll(jnp.broadcast_to(c, (8, 128)), 128 >> lv, 1)[0:1]
            used = lane < (128 >> lv)
            gmc[lv, grows, 128 * h : 128 * h + 128] = jnp.where(used, g, 0.0).astype(BF16)
            cc[lv, :, 128 * h : 128 * h + 128] = jnp.broadcast_to(
                jnp.where(used, c, 0.0), (8, 128)
            )
    remote(
        ra.at[pl.ds(192, 192), pl.ds(256, 256)], pra.at[pl.ds(192, 192), pl.ds(256, 256)],
        cs_sem.at[1], cr_sem.at[1], {"seq": peer},
    ).start()

    def backward(keys, keyst, qm, gm, c_rows, w_ref, dq, n):
        count = keys.shape[0]
        dk = jnp.zeros((count, 256), F32)
        dv = jnp.zeros((count, 256), F32)
        for h in range(3):
            lanes = slice(h * n, h * n + n)
            wb = w_ref[:, lanes]
            inner = nn(keys[:, 128:384], gm[:, lanes])
            slope = (wb.astype(F32) * (inner - c_rows[0:1, lanes])).astype(BF16)
            dq[64 * h : 64 * h + 64, :] += nn(keyst[64 * h : 64 * h + 64, :], slope)
            dk += nt(slope, qm[:, lanes])
            dv += nt(wb, gm[:, lanes])
        return jnp.concatenate(
            [dk[:, 0:128], dk[:, 128:256] + dv[:, 0:128], dv[:, 128:256]], axis=1
        )

    def coarse_backward(lv, i):
        return backward(
            kvc.at[i], kvtc.at[i], qmc.at[lv], gmc.at[lv], cc.at[lv], wc.at[i], dqc.at[lv], 128
        )

    def to_peer(i):
        ownf[i - 3] = coarse_backward(i // 3, i)
        dsendc[i - 3] = ownf[i - 3, pl.ds(other, 64), :].astype(BF16)
        remote(
            dsendc.at[i - 3], sibc.at[i - 3], ss_sem.at[i], sr_sem.at[i], {"seq": peer}
        ).start()

    def return_pair(i):
        lv, j = i // 3, i % 3
        arrived(sibc.at[i - 3], sr_sem.at[i], ss_sem.at[i])
        outc[i - 3] = (
            ownf[i - 3, pl.ds(half, 64), :] + sibc[i - 3].astype(F32)
        ).astype(BF16)
        k = 3 * lv + back_slot(j)
        rows = 128 >> lv
        into = 0 if lv == 1 else lax.rem(s // 2, 2) * 32
        for part in range(parts(lv)):
            remote(
                outc.at[i - 3, pl.ds(part * rows, rows)], retc.at[k - 3, pl.ds(into, rows)],
                bs_sem.at[k], br_sem.at[k], {"seq": target(lv, j, part)},
            ).start()

    def return_first(slot, value):
        out1[slot] = value.astype(BF16)
        where = lax.rem(s + 4 * slot - 2 + 64, 64)
        remote(
            out1.at[slot], ret1.at[1 - slot], bs_sem.at[1 - slot], br_sem.at[1 - slot],
            {"seq": where},
        ).start()

    def near_backward(slot, n, where):
        dsend0[n] = backward(
            kv0.at[slot], kvt0.at[slot], qm0, gm0, c0, w0.at[slot], dq0, 256
        ).astype(BF16)
        remote(dsend0.at[n], ret0.at[n], bs_sem.at[9 + n], br_sem.at[9 + n], {"seq": where}).start()

    near_backward(far, 1, across)
    for i in range(3, 9):
        to_peer(i)
    own1[...] = coarse_backward(0, 2).astype(BF16)
    remote(own1, sib1, ss_sem.at[2], sr_sem.at[2], {"seq": peer}).start()
    for i in range(3, 9):
        return_pair(i)
    return_first(1 - core, coarse_backward(0, 1 - core))
    shared = coarse_backward(0, core)
    arrived(sib1, sr_sem.at[2], ss_sem.at[2])
    return_first(core, shared + sib1[...].astype(F32))
    near_backward(near, 0, peer)
    down[...] = backward(kv0.at[1], kvt0.at[1], qm0, gm0, c0, w0.at[1], dq0, 256)

    def spread(grad, lv):
        if lv == 0:
            return jnp.concatenate([grad, grad], axis=1)
        return grad + pltpu.roll(grad, 128 >> lv, 1)

    grad = round_low(dqc[2] * 0.5)
    for lv in (2, 1, 0):
        grad = unit_back(uc[lv, 0:192, :], grad) * 0.5
        base = dqc[lv - 1] if lv > 0 else dq0[...]
        grad = round_low(base * 0.5) + spread(grad, lv)
    dq_t = unit_back(u0[0:192, :], grad).astype(BF16)
    ra[0:192, 0:256] = dq_t
    remote(
        ra.at[pl.ds(0, 192), pl.ds(0, 256)], pra.at[pl.ds(0, 192), pl.ds(0, 256)],
        cs_sem.at[2], cr_sem.at[2], {"seq": peer},
    ).start()

    att_t = att_s[...]
    for j in range(4):
        mixs[j] = nn(wot[192 * j : 192 * j + 192, :], att_t).astype(BF16)
    for k in range(1, 4):
        remote(
            mixs.at[mp_dev(k)], mixr.at[k - 1], ms_sem.at[k - 1], mr_sem.at[k - 1],
            {"mp": mp_dev(k)},
        ).start()
    for j in range(4):
        gtacc[j] = nn(wqt[192 * j : 192 * j + 192, :], dq_t)

    def widen(blocks):
        at = iota((16 * blocks, 12 * blocks), 0)
        here = (at >> 4) * 12 + (at & 15) == iota((16 * blocks, 12 * blocks), 1)
        return one_hot(here & ((at & 15) < 12))

    first_z = ((z, 8, z_dev, zra, zs_sem, zr_sem, 0), (y, 4, y_dev, yra, ys_sem, yr_sem, 0))
    first_y = ((y, 4, y_dev, yrb, ys_sem, yr_sem, 3), (z, 8, z_dev, zrb, zs_sem, zr_sem, 7))

    def spread_out(src, rows, axis):
        index, count, device, got, send, recv, base = axis
        for k in range(1, count):
            remote(
                src.at[pl.ds(lax.rem(index + k, count) * rows, rows)], got.at[k - 1],
                send.at[base + k - 1], recv.at[base + k - 1], {"seq": device(k)},
            ).start()

    def gathered(own, axis):
        index, count, device, got, send, recv, base = axis
        for k in range(count - 1):
            arrived(got.at[k], recv.at[base + k], send.at[base + k])
            own += got[k].astype(F32)
        return own

    def stage_one(r, total, axes):
        gf[r] = total
        gs[r] = total.astype(BF16)
        spread_out(gs.at[r], 384 // axes[0][1], axes[0])

    def stage_two(r, wide_s, axes):
        rows = 384 // axes[0][1]
        total = gathered(gf[r, pl.ds(axes[0][0] * rows, rows), :], axes[0])
        wide_s[...] = nn(widen(axes[1][1]), total.astype(BF16)).astype(BF16)
        spread_out(wide_s, 16, axes[1])

    def stage_end(wide_s, axes):
        own = wide_s[pl.ds(axes[1][0] * 16, 16), :].astype(F32)
        return gathered(own, axes[1]) * NORM

    arrived(ptg, cr_sem.at[0], cs_sem.at[0])
    arrived(pra.at[pl.ds(192, 192), pl.ds(256, 256)], cr_sem.at[1], cs_sem.at[1])
    arrived(pra.at[pl.ds(0, 192), pl.ds(0, 256)], cr_sem.at[2], cs_sem.at[2])
    stage_one(0, nt(tg[core, :, 0:512], ra[...]) + nt(ptg[:, 0:512], pra[...]), first_z)

    def received(lv):
        if lv == 0:
            total = jnp.zeros((128, 384), F32)
            for i in range(2):
                arrived(ret1.at[i], br_sem.at[i], bs_sem.at[i])
                total += ret1[i].astype(F32)
        else:
            total = jnp.zeros((64, 384), F32)
            for i in range(3 * lv, 3 * lv + 3):
                arrived(retc.at[i - 3], br_sem.at[i], bs_sem.at[i])
                total += retc[i - 3].astype(F32)
            if lv == 2:
                total = total[0:32] + total[32:64]
        total = round_low(total)
        if lv > 0:
            rows = 128 >> lv
            total = jnp.concatenate([total, jnp.zeros((128 - rows, 384), F32)], axis=0)
        return total.T

    total = received(2)
    for lv in (2, 1, 0):
        grad_k = unit_back(uc[lv, 192:384, :], total[0:192]) * 0.5
        grad_v = total[192:384] * ROOT_HALF
        if lv > 0:
            base = received(lv - 1)
        else:
            base = down[...]
            for j in range(2):
                arrived(ret0.at[j], br_sem.at[9 + j], bs_sem.at[9 + j])
                base += ret0[j].astype(F32)
            base = round_low(base).T
        total = base + jnp.concatenate([spread(grad_k, lv), spread(grad_v, lv)], axis=0)
    dkv = jnp.concatenate([unit_back(u0[192:384, :], total[0:192]), total[192:384]], axis=0)
    dkvt[...] = dkv.astype(BF16)
    remote(dkvt, pdkvt, cs_sem.at[3], cr_sem.at[3], {"seq": peer}).start()

    dkv_t = dkvt[...]
    own_part = nt(tg[core, :, 512:768], dkv_t)
    arrived(pdkvt, cr_sem.at[3], cs_sem.at[3])
    stage_one(1, own_part + nt(ptg[:, 512:768], pdkvt[...]), first_y)
    for j in range(4):
        gts[j] = (nn(wkvt[192 * j : 192 * j + 192, :], dkv_t) + gtacc[j]).astype(BF16)
    for k in range(1, 4):
        remote(
            gts.at[mp_dev(k)], gtr.at[k - 1], ms_sem.at[2 + k], mr_sem.at[2 + k],
            {"mp": mp_dev(k)},
        ).start()
    stage_two(0, wsa, first_z)

    def mp_finish(sent, got, base, out):
        total = sent[m].astype(F32)
        for k in range(3):
            arrived(got.at[k], mr_sem.at[base + k], ms_sem.at[base + k])
            total += got[k].astype(F32)
        out[...] = nn(total.astype(BF16), perm_s[...]).astype(BF16)

    mp_finish(mixs, mixr, 0, mixed_ref)
    stage_two(1, wsb, first_y)
    first = stage_end(wsa, first_z)
    go_ref[...] = pltpu.roll(first, 192, 1)[0:12, 0:192]
    gw_ref[:, 0, :] = first[0:12, 0:192]
    mp_finish(gts, gtr, 3, gt_ref)
    second = stage_end(wsb, first_y)
    gw_ref[:, 1, :] = second[0:12, 0:192]
    gw_ref[:, 2, :] = pltpu.roll(second, 192, 1)[0:12, 0:192]

    for i in range(2):
        left(out1.at[i], fs_sem.at[i], fr_sem.at[i])
        left(out1.at[i], bs_sem.at[i], br_sem.at[i])
        left(dsend0.at[i], fs_sem.at[9 + i], fr_sem.at[9 + i])
        left(dsend0.at[i], bs_sem.at[9 + i], br_sem.at[9 + i])
    left(own1, hs_sem.at[2], hr_sem.at[2])
    left(own1, ss_sem.at[2], sr_sem.at[2])
    for i in range(3, 9):
        left(outc.at[i - 3], fs_sem.at[i], fr_sem.at[i])
        left(outc.at[i - 3], hs_sem.at[i], hr_sem.at[i])
        left(outc.at[i - 3], ss_sem.at[i], sr_sem.at[i])
        left(outc.at[i - 3], bs_sem.at[i], br_sem.at[i])
    left(ptg, cs_sem.at[0], cr_sem.at[0])
    left(ra.at[pl.ds(192, 192), pl.ds(256, 256)], cs_sem.at[1], cr_sem.at[1])
    left(ra.at[pl.ds(0, 192), pl.ds(0, 256)], cs_sem.at[2], cr_sem.at[2])
    left(dkvt, cs_sem.at[3], cr_sem.at[3])
    for i in range(6):
        left(mixs.at[0], ms_sem.at[i], mr_sem.at[i])
    for i in range(3):
        left(wsa.at[pl.ds(0, 16)], ys_sem.at[i], yr_sem.at[i])
        left(gs.at[0, pl.ds(0, 96)], ys_sem.at[3 + i], yr_sem.at[3 + i])
    for i in range(7):
        left(gs.at[0, pl.ds(0, 48)], zs_sem.at[i], zr_sem.at[i])
        left(wsa.at[pl.ds(0, 16)], zs_sem.at[7 + i], zr_sem.at[7 + i])


def deliver(*refs):
    count = (len(refs) - 1) // 2
    copies = [
        pltpu.make_async_copy(refs[n], refs[count + n], refs[-1].at[n]) for n in range(count)
    ]
    for copy in copies:
        copy.start()
    for copy in copies:
        copy.wait()


def shards(tokens, w_qkv, w_out, grad_y):
    vmem = pl.BlockSpec(memory_space=pltpu.VMEM)
    hbm = pl.BlockSpec(memory_space=pltpu.HBM)
    low = lambda *shape: pltpu.VMEM(shape, BF16)
    wide = lambda *shape: pltpu.VMEM(shape, F32)
    sems = lambda count: pltpu.SemaphoreType.DMA((count,))
    scratch = [
        low(256, 768), low(576, 768), low(192, 768), low(256, 768),
        low(768, 192), low(768, 192), low(768, 384),
        low(256, 256), wide(576, 256), wide(3, 384, 128),
        low(3, 256, 384), low(9, 128, 384), low(3, 128, 384), low(3, 384, 256), low(9, 384, 128),
        low(3, 256, 768), low(9, 128, 384), low(256, 768), low(3, 256, 384),
        low(256, 768), low(3, 256, 384), wide(8, 768), wide(3, 8, 384),
        wide(192, 256), wide(192, 128), wide(8, 768), wide(8, 384), low(192, 256), low(192, 256),
        wide(192, 256), wide(3, 192, 128), wide(256, 384),
        low(2, 256, 384), low(6, 64, 384), low(2, 256, 384), low(2, 128, 384), low(6, 64, 384),
        low(128, 384), wide(6, 128, 384), low(128, 384), low(6, 64, 384),
        low(2, 128, 384), low(6, 64, 384),
        low(2, 384, 768), low(384, 768), low(384, 512), low(384, 512), low(384, 256), low(384, 256),
        low(4, 192, 256), low(3, 192, 256), wide(4, 192, 256), low(4, 192, 256), low(3, 192, 256),
        wide(2, 384, 384), low(2, 384, 384), low(7, 48, 384), low(3, 16, 384), low(3, 96, 384),
        low(7, 16, 384), low(64, 384), low(128, 384),
        sems(5), sems(11), sems(11), sems(9), sems(9), sems(11), sems(11), sems(9), sems(9),
        sems(4), sems(4), sems(6), sems(6), sems(6), sems(6), sems(14), sems(14),
    ]
    shapes = (
        jax.ShapeDtypeStruct((192, 256), BF16),
        jax.ShapeDtypeStruct((192, 256), BF16),
        jax.ShapeDtypeStruct((12, 3, 192), F32),
        jax.ShapeDtypeStruct((12, 192), F32),
    )
    results = pl.pallas_call(
        kernel,
        out_shape=shapes,
        in_specs=[hbm] * 4,
        out_specs=(vmem,) * 4,
        scratch_shapes=scratch,
        compiler_params=pltpu.CompilerParams(
            collective_id=0, has_side_effects=True, vmem_limit_bytes=56098816
        ),
        cost_estimate=pl.CostEstimate(
            flops=2_000_000_000, bytes_accessed=4_000_000, transcendentals=1_000_000
        ),
    )(
        tokens.reshape(256, 768), w_qkv.reshape(576, 768), w_out, grad_y.reshape(256, 768)
    )
    mixed, grad_tokens, grad_wqkv, grad_wout = pl.pallas_call(
        deliver,
        out_shape=shapes,
        in_specs=[vmem] * 4,
        out_specs=(hbm,) * 4,
        scratch_shapes=[sems(4)],
        compiler_params=pltpu.CompilerParams(vmem_limit_bytes=1024 * 1024),
    )(*results)
    return (mixed.T[None], grad_tokens.T[None], grad_wqkv, grad_wout)


def solution(mesh):
    in_specs = (P(None, "seq", None), P(None, "mp", None), P("mp", None), P(None, "seq", None))
    out_specs = (P(None, "seq", "mp"), P(None, "seq", "mp"), P("seq", None, "mp"), P("seq", "mp"))
    return jax.shard_map(shards, mesh=mesh, in_specs=in_specs, out_specs=out_specs, check_vma=False)
```

```python
import jax
import jax.numpy as jnp
from jax import lax
from jax.experimental import pallas as pl
from jax.experimental.pallas import tpu as pltpu
from jax.sharding import PartitionSpec as P

F32 = jnp.float32
BF16 = jnp.bfloat16
MESH = pl.DeviceIdType.MESH
EPS = 1e-06
ROOT_HALF = 0.7071067811865476
NORM = 1.0 / 128.0


def nn(a, b):
    return jnp.dot(a, b, preferred_element_type=F32)


def nt(a, b):
    return lax.dot_general(a, b, (((1,), (1,)), ((), ())), preferred_element_type=F32)


def unit_parts(x):
    heads = x.reshape(x.shape[0] // 64, 64, x.shape[1])
    scale = lax.rsqrt(jnp.mean(heads * heads, axis=1, keepdims=True) + EPS)
    return heads * scale, scale


def unit(x):
    return unit_parts(x)[0].reshape(x.shape)


def unit_back(x, grad):
    y, scale = unit_parts(x)
    dy = grad.reshape(y.shape)
    return (scale * (dy - y * jnp.mean(y * dy, axis=1, keepdims=True))).reshape(x.shape)


def round_low(x):
    return x.astype(BF16).astype(F32)


def iota(shape, dim):
    return lax.broadcasted_iota(jnp.int32, shape, dim)


def one_hot(cond):
    return jnp.where(cond, 1.0, 0.0).astype(BF16)


def natural_token(row):
    high = row >> 5
    return (row & 31) * 8 + (((high & 1) << 2) | (high & 2) | ((high >> 2) & 1))


def kernel(
    tok_hbm, wqkv_hbm, wout_hbm, gy_hbm,
    mixed_ref, gt_ref, gw_ref, go_ref,
    tok_ref, wqkv_ref, wout_ref, gy_ref, wot, wqt, wkvt,
    perm_s, u0, uc, kv0, kvc, ownc, kvt0, kvtc, w0, wc, qm0, qmc, gm0, gmc, c0, cc,
    num0, numc, den0, denc, dot_s, att_s, dq0, dqc, down, dsend0, dsendc, ret0, ret1, retc,
    own1, own1f, ownf, sib1, sibc, out1, outc,
    tg, ptg, ra, pra, dkvt, pdkvt, mixs, mixr, gtacc, gts, gtr,
    gfa, gsa, wsa, zra, yra, gfb, gsb, wsb, yrb, zrb, gfc, gsc, wsc, zrc, yrc,
    in_sem, fs_sem, fr_sem, hs_sem, hr_sem, bs_sem, br_sem, ss_sem, sr_sem,
    cs_sem, cr_sem, ms_sem, mr_sem, ys_sem, yr_sem, zs_sem, zr_sem,
):
    loads = [
        pltpu.make_async_copy(src, dst, in_sem.at[n])
        for n, (src, dst) in enumerate((
            (tok_hbm, tok_ref),
            (wqkv_hbm.at[pl.ds(192, 384)], wqkv_ref.at[pl.ds(192, 384)]),
            (wqkv_hbm.at[pl.ds(0, 192)], wqkv_ref.at[pl.ds(0, 192)]),
            (gy_hbm, gy_ref),
            (wout_hbm, wout_ref),
        ))
    ]
    for load in loads:
        load.start()

    s = lax.axis_index("seq")
    m = lax.axis_index("mp")
    core = lax.rem(s, 2)
    y = lax.rem(s // 2, 4)
    z = s // 8
    position = (s, s // 2, s // 4)
    extent = (64, 32, 16)
    skip = [3 - 6 * lax.rem(position[lv], 2) for lv in range(3)]

    def offset(lv, j):
        return (-2, 2, skip[lv])[j]

    def target(lv, j, part):
        block = lax.rem(position[lv] + offset(lv, j) + extent[lv], extent[lv])
        return block if lv == 0 else block * (1 << lv) + 2 * part + core

    def parts(lv):
        return 2 if lv == 2 else 1

    def back_slot(j):
        return (1, 0, 2)[j]

    prev_dev = lax.rem(s + 63, 64)
    next_dev = lax.rem(s + 1, 64)
    peer = s + 1 - 2 * core
    across = lax.rem(s + 2 * core + 63, 64)

    def y_dev(k):
        return z * 8 + lax.rem(y + k, 4) * 2 + core

    def z_dev(k):
        return lax.rem(z + k, 8) * 8 + y * 2 + core

    def mp_dev(k):
        return lax.rem(m + k, 4)

    barrier = pltpu.get_barrier_semaphore()
    partners = [{"seq": prev_dev}, {"seq": next_dev}]
    for lv in range(3):
        for j in range(2 if lv == 0 else 3):
            for part in range(parts(lv)):
                partners.append({"seq": target(lv, j, part)})
    partners += [{"seq": y_dev(k)} for k in range(1, 4)]
    partners += [{"seq": z_dev(k)} for k in range(1, 8)]
    partners += [{"mp": mp_dev(k)} for k in range(1, 4)]
    for partner in partners:
        pl.semaphore_signal(barrier, inc=1, device_id=partner, device_id_type=MESH)

    def remote(src, dst, send, recv, where):
        return pltpu.make_async_remote_copy(
            src_ref=src, dst_ref=dst, send_sem=send, recv_sem=recv,
            device_id=where, device_id_type=MESH,
        )

    def arrived(ref, sem, spare):
        remote(ref, ref, spare, sem, {"seq": peer}).wait_recv()

    def left(ref, sem, spare):
        remote(ref, ref, sem, spare, {"seq": peer}).wait_send()

    perm = one_hot(natural_token(iota((256, 256), 0)) == iota((256, 256), 1))
    perm_s[...] = perm
    loads[0].wait()
    tok_p = nn(perm, tok_ref[...]).astype(BF16)
    loads[1].wait()
    u0[192:576, :] = nt(wqkv_ref[192:576, :], tok_p)

    def halves(x, lv):
        return x[:, 0:128] + x[:, 128:256] if lv == 0 else x + pltpu.roll(x, 128 >> lv, 1)

    key = unit(u0[192:384, :])
    v = u0[384:576, :]
    kv0[1] = jnp.concatenate([key, v], axis=0).T.astype(BF16)
    pl.semaphore_wait(barrier, len(partners))

    remote(kv0.at[1], kv0.at[2 * core], fs_sem.at[9], fr_sem.at[9], {"seq": peer}).start()
    remote(kv0.at[1], kv0.at[2 - 2 * core], fs_sem.at[10], fr_sem.at[10], {"seq": across}).start()
    for lv in range(3):
        mean = halves(key, lv) * 0.5
        v = halves(v, lv) * ROOT_HALF
        uc[lv, 192:384, :] = mean
        key = unit(mean)
        ownc[lv] = jnp.concatenate([key, v], axis=0).T.astype(BF16)

    mine = (0, core * 64, core * 64 + lax.rem(s // 2, 2) * 32)
    for lv in (2, 1, 0):
        rows = 128 >> lv
        for j in range(2 if lv == 0 else 3):
            i = 3 * lv + back_slot(j)
            for part in range(parts(lv)):
                remote(
                    ownc.at[lv, pl.ds(0, rows)],
                    kvc.at[i, pl.ds(mine[lv], rows)],
                    fs_sem.at[i], fr_sem.at[i], {"seq": target(lv, j, part)},
                ).start()
    def store_q(dst, q_rows, n):
        dst[...] = jnp.zeros(dst.shape, BF16)
        half = (q_rows * 0.5).astype(BF16)
        for h in range(3):
            dst[64 * h : 64 * h + 64, h * n : h * n + n] = half[64 * h : 64 * h + 64]

    loads[2].wait()
    u0[0:192, :] = nt(wqkv_ref[0:192, :], tok_p)
    query = unit(u0[0:192, :])
    store_q(qm0, query, 256)
    for lv in range(3):
        mean = halves(query, lv) * 0.5
        uc[lv, 0:192, :] = mean
        query = unit(mean)
        store_q(qmc.at[lv], query, 128)

    num0[...] = jnp.zeros(num0.shape, F32)
    numc[...] = jnp.zeros(numc.shape, F32)
    den0[...] = jnp.zeros(den0.shape, F32)
    denc[...] = jnp.zeros(denc.shape, F32)
    dq0[...] = jnp.zeros(dq0.shape, F32)
    dqc[...] = jnp.zeros(dqc.shape, F32)
    ra[...] = jnp.zeros(ra.shape, BF16)
    pra[0:192, 256:512] = jnp.zeros((192, 256), BF16)
    pra[192:384, 0:256] = jnp.zeros((192, 256), BF16)

    def forward(block, factors, keyst, qm, w_ref, num, den, n):
        count = block.shape[0]
        step = count // len(factors)
        turned = block.astype(F32).T.astype(BF16)
        keyst[...] = turned
        w = jnp.exp(nn(block[:, 0:256], qm[...]))
        w = jnp.concatenate(
            [w[step * k : step * k + step] * factor for k, factor in enumerate(factors)], axis=0
        )
        den[...] += jnp.sum(w.reshape(count // 8, 8, 3 * n), axis=0)
        wb = w.astype(BF16)
        w_ref[...] = wb
        for h in range(3):
            num[64 * h : 64 * h + 64, :] += nn(
                turned[192 + 64 * h : 256 + 64 * h], wb[:, h * n : h * n + n]
            )

    def near_forward(slot, factor):
        forward(kv0[slot], [factor], kvt0.at[slot], qm0, w0.at[slot], num0, den0, 256)

    near, far = 2 - 2 * core, 2 * core
    outside = ((s == 0) & (core == 0)) | ((s == 63) & (core == 1))
    far_keep = jnp.where(outside, jnp.float32(0.0), jnp.float32(1.0))
    one = jnp.float32(1.0)
    near_forward(1, one)

    loads[3].wait()
    loads[4].wait()
    gy_p = nn(perm, gy_ref[...]).astype(BF16)
    dot_s[...] = nt(wout_ref[...], gy_p).astype(BF16)
    for half in range(2):
        index = iota((384, 768), 0)
        twelfth = (index * 5462) >> 16
        rest = half * 12 + (index - 12 * twelfth)
        feature = (twelfth >> 2) * 96 + (twelfth & 3) * 24 + rest
        pick = one_hot(feature == iota((384, 768), 1))
        tg[half, :, 0:256] = nt(pick, tok_p).astype(BF16)
        tg[half, :, 256:512] = nt(pick, gy_p).astype(BF16)
        feature = (twelfth & 7) * 96 + (twelfth >> 3) * 24 + rest
        pick = one_hot(feature == iota((384, 768), 1))
        tg[half, :, 512:768] = nt(pick, tok_p).astype(BF16)
    remote(tg.at[1 - core], ptg, cs_sem.at[0], cr_sem.at[0], {"seq": peer}).start()

    arrived(kv0.at[near], fr_sem.at[9], fs_sem.at[9])
    near_forward(near, one)

    same = one_hot(iota((256, 256), 0) == iota((256, 256), 1))
    for n in range(3):
        cut = slice(256 * n, 256 * n + 256)
        wot[cut, :] = nt(same, wout_ref[:, cut]).astype(BF16)
        wqt[cut, :] = nt(same, wqkv_ref[0:192, cut]).astype(BF16)
        wkvt[cut, :] = nt(same, wqkv_ref[192:576, cut]).astype(BF16)

    half = core * 64
    other = 64 - half
    arrived(kv0.at[far], fr_sem.at[10], fs_sem.at[10])
    near_forward(far, far_keep)
    for i in range(3, 9):
        piece = kvc.at[i, pl.ds(half, 64)]
        arrived(piece, fr_sem.at[i], fs_sem.at[i])
        remote(piece, piece, hs_sem.at[i], hr_sem.at[i], {"seq": peer}).start()
    arrived(kvc.at[0], fr_sem.at[0], fs_sem.at[0])
    arrived(kvc.at[1], fr_sem.at[1], fs_sem.at[1])
    remote(kvc.at[core], kvc.at[2], hs_sem.at[2], hr_sem.at[2], {"seq": peer}).start()

    def coarse_forward(lv):
        factors = []
        for j in range(3):
            place = position[lv] + offset(lv, j)
            inside = (place >= 0) & (place < extent[lv])
            factors.append(jnp.where(inside, jnp.float32(2 << lv), jnp.float32(0.0)))
        block = kvc[3 * lv : 3 * lv + 3].reshape(384, 384)
        forward(block, factors, kvtc.at[lv], qmc.at[lv], wc.at[lv], numc, denc, 128)

    for lv in (2, 1):
        for i in range(3 * lv, 3 * lv + 3):
            arrived(kvc.at[i, pl.ds(other, 64)], hr_sem.at[i], hs_sem.at[i])
        coarse_forward(lv)
    arrived(kvc.at[2], hr_sem.at[2], hs_sem.at[2])
    coarse_forward(0)

    lane = iota((1, 128), 1)
    gm0[...] = jnp.zeros(gm0.shape, BF16)
    gmc[...] = jnp.zeros(gmc.shape, BF16)
    for h in range(3):
        rows = slice(64 * h, 64 * h + 64)
        grows = slice(64 * h + 64, 64 * h + 128)
        coarse = jnp.sum(denc[:, 128 * h : 128 * h + 128], axis=0, keepdims=True)
        den = jnp.sum(den0[:, 256 * h : 256 * h + 256], axis=0, keepdims=True)
        inverse = 1.0 / (den + jnp.concatenate([coarse, coarse], axis=1))
        more = numc[rows, :]
        att = ((num0[rows, :] + jnp.concatenate([more, more], axis=1)) * inverse).astype(BF16)
        ra[192 + 64 * h : 256 + 64 * h, 256:512] = att
        att_s[rows, :] = att
        d_att = dot_s[rows, :].astype(F32)
        g = d_att * inverse
        c = jnp.sum(d_att * att.astype(F32), axis=0, keepdims=True) * inverse
        gm0[grows, 256 * h : 256 * h + 256] = g.astype(BF16)
        c0[:, 256 * h : 256 * h + 256] = jnp.broadcast_to(c, (8, 256))
        g = g[:, 0:128] + g[:, 128:256]
        c = c[:, 0:128] + c[:, 128:256]
        for lv in range(3):
            if lv > 0:
                g = g + pltpu.roll(g, 128 >> lv, 1)
                c = c + pltpu.roll(jnp.broadcast_to(c, (8, 128)), 128 >> lv, 1)[0:1]
            used = lane < (128 >> lv)
            gmc[lv, grows, 128 * h : 128 * h + 128] = jnp.where(used, g, 0.0).astype(BF16)
            cc[lv, :, 128 * h : 128 * h + 128] = jnp.broadcast_to(
                jnp.where(used, c, 0.0), (8, 128)
            )
    remote(
        ra.at[pl.ds(192, 192), pl.ds(256, 256)], pra.at[pl.ds(192, 192), pl.ds(256, 256)],
        cs_sem.at[1], cr_sem.at[1], {"seq": peer},
    ).start()

    def backward(block, keyst, qm, gm, c_rows, w_ref, dq, n):
        wb = w_ref[...]
        inner = nn(block[:, 128:384], gm[...])
        slope = (wb.astype(F32) * (inner - c_rows[0:1, :])).astype(BF16)
        dk = nt(slope, qm[...])
        dv = nt(wb, gm[...])
        for h in range(3):
            dq[64 * h : 64 * h + 64, :] += nn(
                keyst[64 * h : 64 * h + 64, :], slope[:, h * n : h * n + n]
            )
        return jnp.concatenate(
            [dk[:, 0:128], dk[:, 128:256] + dv[:, 0:128], dv[:, 128:256]], axis=1
        )

    def coarse_backward(lv):
        block = kvc[3 * lv : 3 * lv + 3].reshape(384, 384)
        return backward(
            block, kvtc.at[lv], qmc.at[lv], gmc.at[lv], cc.at[lv], wc.at[lv], dqc.at[lv], 128
        )

    def to_peer(lv):
        ownf[lv - 1] = coarse_backward(lv).reshape(3, 2, 64, 384)
        dsendc[lv - 1] = ownf[lv - 1, :, 1 - core].astype(BF16)
        remote(
            dsendc.at[lv - 1], sibc.at[lv - 1], ss_sem.at[lv], sr_sem.at[lv], {"seq": peer}
        ).start()

    def return_pairs(lv):
        arrived(sibc.at[lv - 1], sr_sem.at[lv], ss_sem.at[lv])
        outc[lv - 1] = (ownf[lv - 1, :, core] + sibc[lv - 1].astype(F32)).astype(BF16)
        rows = 128 >> lv
        into = 0 if lv == 1 else lax.rem(s // 2, 2) * 32
        for j in range(3):
            k = 3 * lv + back_slot(j)
            for part in range(parts(lv)):
                remote(
                    outc.at[lv - 1, j, pl.ds(part * rows, rows)], retc.at[k - 3, pl.ds(into, rows)],
                    bs_sem.at[k], br_sem.at[k], {"seq": target(lv, j, part)},
                ).start()

    def return_first(slot, value):
        out1[slot] = value.astype(BF16)
        where = lax.rem(s + 4 * slot - 2 + 64, 64)
        remote(
            out1.at[slot], ret1.at[1 - slot], bs_sem.at[1 - slot], br_sem.at[1 - slot],
            {"seq": where},
        ).start()

    def near_backward(slot):
        return backward(kv0[slot], kvt0.at[slot], qm0, gm0, c0, w0.at[slot], dq0, 256)

    def return_near(slot, n, where):
        dsend0[n] = near_backward(slot).astype(BF16)
        remote(dsend0.at[n], ret0.at[n], bs_sem.at[9 + n], br_sem.at[9 + n], {"seq": where}).start()

    return_near(far, 1, across)
    to_peer(2)
    to_peer(1)
    own1f[...] = coarse_backward(0).reshape(3, 128, 384)
    own1[...] = own1f[2].astype(BF16)
    remote(own1, sib1, ss_sem.at[0], sr_sem.at[0], {"seq": peer}).start()
    return_pairs(2)
    return_pairs(1)
    return_first(1 - core, own1f[1 - core])
    arrived(sib1, sr_sem.at[0], ss_sem.at[0])
    return_first(core, own1f[core] + sib1[...].astype(F32))
    return_near(near, 0, peer)
    down[...] = near_backward(1)

    def spread(grad, lv):
        if lv == 0:
            return jnp.concatenate([grad, grad], axis=1)
        return grad + pltpu.roll(grad, 128 >> lv, 1)

    grad = round_low(dqc[2] * 0.5)
    for lv in (2, 1, 0):
        grad = unit_back(uc[lv, 0:192, :], grad) * 0.5
        base = dqc[lv - 1] if lv > 0 else dq0[...]
        grad = round_low(base * 0.5) + spread(grad, lv)
    dq_t = unit_back(u0[0:192, :], grad).astype(BF16)
    ra[0:192, 0:256] = dq_t
    remote(
        ra.at[pl.ds(0, 192), pl.ds(0, 256)], pra.at[pl.ds(0, 192), pl.ds(0, 256)],
        cs_sem.at[2], cr_sem.at[2], {"seq": peer},
    ).start()

    att_t = att_s[...]
    for j in range(4):
        mixs[j] = nn(wot[192 * j : 192 * j + 192, :], att_t).astype(BF16)
    for k in range(1, 4):
        remote(
            mixs.at[mp_dev(k)], mixr.at[k - 1], ms_sem.at[k - 1], mr_sem.at[k - 1],
            {"mp": mp_dev(k)},
        ).start()
    for j in range(4):
        gtacc[j] = nn(wqt[192 * j : 192 * j + 192, :], dq_t)

    def widen(blocks):
        at = iota((16 * blocks, 12 * blocks), 0)
        here = (at >> 4) * 12 + (at & 15) == iota((16 * blocks, 12 * blocks), 1)
        return one_hot(here & ((at & 15) < 12))

    part_a = (
        gfa, gsa, wsa,
        ((z, 8, z_dev, zra, zs_sem, zr_sem, 0), (y, 4, y_dev, yra, ys_sem, yr_sem, 0)),
    )
    part_b = (
        gfb, gsb, wsb,
        ((y, 4, y_dev, yrb, ys_sem, yr_sem, 3), (z, 8, z_dev, zrb, zs_sem, zr_sem, 7)),
    )
    part_c = (
        gfc, gsc, wsc,
        ((z, 8, z_dev, zrc, zs_sem, zr_sem, 14), (y, 4, y_dev, yrc, ys_sem, yr_sem, 6)),
    )

    def spread_out(src, rows, axis):
        index, count, device, got, send, recv, base = axis
        for k in range(1, count):
            remote(
                src.at[pl.ds(lax.rem(index + k, count) * rows, rows)], got.at[k - 1],
                send.at[base + k - 1], recv.at[base + k - 1], {"seq": device(k)},
            ).start()

    def gathered(own, axis):
        index, count, device, got, send, recv, base = axis
        for k in range(count - 1):
            arrived(got.at[k], recv.at[base + k], send.at[base + k])
            own += got[k].astype(F32)
        return own

    def stage_one(part, total):
        whole, low_s, wide_s, axes = part
        whole[...] = total
        low_s[...] = total.astype(BF16)
        spread_out(low_s, 384 // axes[0][1], axes[0])

    def stage_two(part):
        whole, low_s, wide_s, axes = part
        rows = 384 // axes[0][1]
        total = gathered(whole[pl.ds(axes[0][0] * rows, rows), :], axes[0])
        wide_s[...] = nn(widen(axes[1][1]), total.astype(BF16)).astype(BF16)
        spread_out(wide_s, 16, axes[1])

    def stage_end(part):
        whole, low_s, wide_s, axes = part
        own = wide_s[pl.ds(axes[1][0] * 16, 16), :].astype(F32)
        return gathered(own, axes[1]) * NORM

    def stage_left(part):
        whole, low_s, wide_s, axes = part
        for rows, src, axis in ((384 // axes[0][1], low_s, axes[0]), (16, wide_s, axes[1])):
            index, count, device, got, send, recv, base = axis
            for k in range(count - 1):
                left(src.at[pl.ds(0, rows)], send.at[base + k], recv.at[base + k])

    arrived(ptg, cr_sem.at[0], cs_sem.at[0])
    arrived(pra.at[pl.ds(192, 192), pl.ds(256, 256)], cr_sem.at[1], cs_sem.at[1])
    arrived(pra.at[pl.ds(0, 192), pl.ds(0, 256)], cr_sem.at[2], cs_sem.at[2])
    stage_one(part_a, nt(tg[core, :, 0:512], ra[...]) + nt(ptg[:, 0:512], pra[...]))

    def received(lv):
        if lv == 0:
            total = jnp.zeros((128, 384), F32)
            for i in range(2):
                arrived(ret1.at[i], br_sem.at[i], bs_sem.at[i])
                total += ret1[i].astype(F32)
        else:
            total = jnp.zeros((64, 384), F32)
            for i in range(3 * lv, 3 * lv + 3):
                arrived(retc.at[i - 3], br_sem.at[i], bs_sem.at[i])
                total += retc[i - 3].astype(F32)
            if lv == 2:
                total = total[0:32] + total[32:64]
        total = round_low(total)
        if lv > 0:
            rows = 128 >> lv
            total = jnp.concatenate([total, jnp.zeros((128 - rows, 384), F32)], axis=0)
        return total.T

    total = received(2)
    for lv in (2, 1, 0):
        grad_k = unit_back(uc[lv, 192:384, :], total[0:192]) * 0.5
        grad_v = total[192:384] * ROOT_HALF
        if lv > 0:
            base = received(lv - 1)
        else:
            base = down[...]
            for j in range(2):
                arrived(ret0.at[j], br_sem.at[9 + j], bs_sem.at[9 + j])
                base += ret0[j].astype(F32)
            base = round_low(base).T
        total = base + jnp.concatenate([spread(grad_k, lv), spread(grad_v, lv)], axis=0)
    dkv = jnp.concatenate([unit_back(u0[192:384, :], total[0:192]), total[192:384]], axis=0)
    dkvt[...] = dkv.astype(BF16)
    remote(dkvt, pdkvt, cs_sem.at[3], cr_sem.at[3], {"seq": peer}).start()

    dkv_t = dkvt[...]
    own_b = nt(tg[core, :, 512:768], dkv_t[0:256])
    own_c = nt(tg[core, :, 0:256], dkv_t[256:384])
    arrived(pdkvt, cr_sem.at[3], cs_sem.at[3])
    stage_one(part_b, own_b + nt(ptg[:, 512:768], pdkvt[0:256, :]))
    stage_one(part_c, own_c + nt(ptg[:, 0:256], pdkvt[256:384, :]))
    for j in range(4):
        gts[j] = (nn(wkvt[192 * j : 192 * j + 192, :], dkv_t) + gtacc[j]).astype(BF16)
    for k in range(1, 4):
        remote(
            gts.at[mp_dev(k)], gtr.at[k - 1], ms_sem.at[2 + k], mr_sem.at[2 + k],
            {"mp": mp_dev(k)},
        ).start()
    stage_two(part_a)

    def mp_finish(sent, got, base, out):
        total = sent[m].astype(F32)
        for k in range(3):
            arrived(got.at[k], mr_sem.at[base + k], ms_sem.at[base + k])
            total += got[k].astype(F32)
        out[...] = nn(total.astype(BF16), perm_s[...]).astype(BF16)

    mp_finish(mixs, mixr, 0, mixed_ref)
    stage_two(part_b)
    stage_two(part_c)
    first = stage_end(part_a)
    go_ref[...] = pltpu.roll(first, 192, 1)[0:12, 0:192]
    gw_ref[:, 0, :] = first[0:12, 0:192]
    mp_finish(gts, gtr, 3, gt_ref)
    third = stage_end(part_c)
    second = jnp.concatenate([stage_end(part_b), third], axis=1)
    gw_ref[:, 1, :] = second[0:12, 0:192]
    gw_ref[:, 2, :] = pltpu.roll(second, 192, 1)[0:12, 0:192]

    for i in range(2):
        left(out1.at[i], fs_sem.at[i], fr_sem.at[i])
        left(out1.at[i], bs_sem.at[i], br_sem.at[i])
        left(dsend0.at[i], fs_sem.at[9 + i], fr_sem.at[9 + i])
        left(dsend0.at[i], bs_sem.at[9 + i], br_sem.at[9 + i])
    left(own1, hs_sem.at[2], hr_sem.at[2])
    left(own1, ss_sem.at[0], sr_sem.at[0])
    for lv in (1, 2):
        left(dsendc.at[0], ss_sem.at[lv], sr_sem.at[lv])
    for i in range(3, 9):
        left(outc.at[0, 0], fs_sem.at[i], fr_sem.at[i])
        left(outc.at[0, 0], hs_sem.at[i], hr_sem.at[i])
        left(outc.at[0, 0], bs_sem.at[i], br_sem.at[i])
    left(ptg, cs_sem.at[0], cr_sem.at[0])
    left(ra.at[pl.ds(192, 192), pl.ds(256, 256)], cs_sem.at[1], cr_sem.at[1])
    left(ra.at[pl.ds(0, 192), pl.ds(0, 256)], cs_sem.at[2], cr_sem.at[2])
    left(dkvt, cs_sem.at[3], cr_sem.at[3])
    for i in range(6):
        left(mixs.at[0], ms_sem.at[i], mr_sem.at[i])
    for part in (part_a, part_b, part_c):
        stage_left(part)


def deliver(*refs):
    count = (len(refs) - 1) // 2
    copies = [
        pltpu.make_async_copy(refs[n], refs[count + n], refs[-1].at[n]) for n in range(count)
    ]
    for copy in copies:
        copy.start()
    for copy in copies:
        copy.wait()


def shards(tokens, w_qkv, w_out, grad_y):
    vmem = pl.BlockSpec(memory_space=pltpu.VMEM)
    hbm = pl.BlockSpec(memory_space=pltpu.HBM)
    low = lambda *shape: pltpu.VMEM(shape, BF16)
    wide = lambda *shape: pltpu.VMEM(shape, F32)
    sems = lambda count: pltpu.SemaphoreType.DMA((count,))
    scratch = [
        low(256, 768), low(576, 768), low(192, 768), low(256, 768),
        low(768, 192), low(768, 192), low(768, 384),
        low(256, 256), wide(576, 256), wide(3, 384, 128),
        low(3, 256, 384), low(9, 128, 384), low(3, 128, 384), low(3, 384, 256), low(3, 384, 384),
        low(3, 256, 768), low(3, 384, 384), low(256, 768), low(3, 256, 384),
        low(256, 768), low(3, 256, 384), wide(8, 768), wide(3, 8, 384),
        wide(192, 256), wide(192, 128), wide(8, 768), wide(8, 384), low(192, 256), low(192, 256),
        wide(192, 256), wide(3, 192, 128), wide(256, 384),
        low(2, 256, 384), low(2, 3, 64, 384), low(2, 256, 384), low(2, 128, 384), low(6, 64, 384),
        low(128, 384), wide(3, 128, 384), wide(2, 3, 2, 64, 384), low(128, 384), low(2, 3, 64, 384),
        low(2, 128, 384), low(2, 3, 64, 384),
        low(2, 384, 768), low(384, 768), low(384, 512), low(384, 512), low(384, 256), low(384, 256),
        low(4, 192, 256), low(3, 192, 256), wide(4, 192, 256), low(4, 192, 256), low(3, 192, 256),
        wide(384, 384), low(384, 384), low(64, 384), low(7, 48, 384), low(3, 16, 384),
        wide(384, 256), low(384, 256), low(128, 256), low(3, 96, 256), low(7, 16, 256),
        wide(384, 128), low(384, 128), low(64, 128), low(7, 48, 128), low(3, 16, 128),
        sems(5), sems(11), sems(11), sems(9), sems(9), sems(11), sems(11), sems(3), sems(3),
        sems(4), sems(4), sems(6), sems(6), sems(9), sems(9), sems(21), sems(21),
    ]
    shapes = (
        jax.ShapeDtypeStruct((192, 256), BF16),
        jax.ShapeDtypeStruct((192, 256), BF16),
        jax.ShapeDtypeStruct((12, 3, 192), F32),
        jax.ShapeDtypeStruct((12, 192), F32),
    )
    results = pl.pallas_call(
        kernel,
        out_shape=shapes,
        in_specs=[hbm] * 4,
        out_specs=(vmem,) * 4,
        scratch_shapes=scratch,
        compiler_params=pltpu.CompilerParams(
            collective_id=0, has_side_effects=True, vmem_limit_bytes=56098816
        ),
        cost_estimate=pl.CostEstimate(
            flops=2_000_000_000, bytes_accessed=4_000_000, transcendentals=1_000_000
        ),
    )(
        tokens.reshape(256, 768), w_qkv.reshape(576, 768), w_out, grad_y.reshape(256, 768)
    )
    mixed, grad_tokens, grad_wqkv, grad_wout = pl.pallas_call(
        deliver,
        out_shape=shapes,
        in_specs=[vmem] * 4,
        out_specs=(hbm,) * 4,
        scratch_shapes=[sems(4)],
        compiler_params=pltpu.CompilerParams(vmem_limit_bytes=1024 * 1024),
    )(*results)
    return (mixed.T[None], grad_tokens.T[None], grad_wqkv, grad_wout)


def solution(mesh):
    in_specs = (P(None, "seq", None), P(None, "mp", None), P("mp", None), P(None, "seq", None))
    out_specs = (P(None, "seq", "mp"), P(None, "seq", "mp"), P("seq", None, "mp"), P("seq", "mp"))
    return jax.shard_map(shards, mesh=mesh, in_specs=in_specs, out_specs=out_specs, check_vma=False)
```

```python
import jax
import jax.numpy as jnp
from jax import lax
from jax.experimental import pallas as pl
from jax.experimental.pallas import tpu as pltpu
from jax.sharding import PartitionSpec as P

F32 = jnp.float32
BF16 = jnp.bfloat16
MESH = pl.DeviceIdType.MESH
EPS = 1e-06
ROOT_HALF = 0.7071067811865476
NORM = 1.0 / 128.0


def nn(a, b):
    return jnp.dot(a, b, preferred_element_type=F32)


def nt(a, b):
    return lax.dot_general(a, b, (((1,), (1,)), ((), ())), preferred_element_type=F32)


def unit_parts(x):
    heads = x.reshape(x.shape[0] // 64, 64, x.shape[1])
    scale = lax.rsqrt(jnp.mean(heads * heads, axis=1, keepdims=True) + EPS)
    return heads * scale, scale


def unit(x):
    return unit_parts(x)[0].reshape(x.shape)


def unit_back(x, grad):
    y, scale = unit_parts(x)
    dy = grad.reshape(y.shape)
    return (scale * (dy - y * jnp.mean(y * dy, axis=1, keepdims=True))).reshape(x.shape)


def round_low(x):
    return x.astype(BF16).astype(F32)


def iota(shape, dim):
    return lax.broadcasted_iota(jnp.int32, shape, dim)


def one_hot(cond):
    return jnp.where(cond, 1.0, 0.0).astype(BF16)


def natural_token(row):
    high = row >> 5
    return (row & 31) * 8 + (((high & 1) << 2) | (high & 2) | ((high >> 2) & 1))


def kernel(
    tok_hbm, wqkv_hbm, wout_hbm, gy_hbm,
    mixed_ref, gt_ref, gw_ref, go_ref,
    tok_ref, wqkv_ref, wout_ref, gy_ref, wot, wqt, wkvt,
    perm_s, u0, uc, kv0, kvc, ownc, kvt0, kvtc, w0, wc, qm0, qmc, gm0, gmc, c0, cc,
    num0, numc, den0, denc, dot_s, att_s, dq0, dqc, down, dsend0, dsendc, ret0, retc,
    ownf, sibc, outc,
    q0s, q1s, q0r, q1r, g0s, g1s, g0r, g1r, qmr0, gmr0, qmr1, gmr1,
    tg, ptg, ra, pra, dkvt, pdkvt, mixs, mixr, gtacc, gts, gtr,
    gfa, gsa, wsa, zra, yra, gfb, gsb, wsb, yrb, zrb, gfc, gsc, wsc, zrc, yrc,
    in_sem, fs_sem, fr_sem, hs_sem, hr_sem, bs_sem, br_sem, ss_sem, sr_sem,
    qs_sem, qr_sem, cs_sem, cr_sem, ms_sem, mr_sem, ys_sem, yr_sem, zs_sem, zr_sem,
):
    loads = [
        pltpu.make_async_copy(src, dst, in_sem.at[n])
        for n, (src, dst) in enumerate((
            (tok_hbm, tok_ref),
            (wqkv_hbm.at[pl.ds(192, 384)], wqkv_ref.at[pl.ds(192, 384)]),
            (wqkv_hbm.at[pl.ds(0, 192)], wqkv_ref.at[pl.ds(0, 192)]),
            (gy_hbm, gy_ref),
            (wout_hbm, wout_ref),
        ))
    ]
    for load in loads:
        load.start()

    s = lax.axis_index("seq")
    m = lax.axis_index("mp")
    core = lax.rem(s, 2)
    y = lax.rem(s // 2, 4)
    z = s // 8
    position = (s, s // 2, s // 4)
    extent = (64, 32, 16)
    skip = [3 - 6 * lax.rem(position[lv], 2) for lv in range(3)]

    def offset(lv, j):
        return (-2, 2, skip[lv])[j]

    def target(lv, j, part):
        block = lax.rem(position[lv] + offset(lv, j) + extent[lv], extent[lv])
        return block if lv == 0 else block * (1 << lv) + 2 * part + core

    def parts(lv):
        return 2 if lv == 2 else 1

    def back_slot(j):
        return (1, 0, 2)[j]

    prev_dev = lax.rem(s + 63, 64)
    next_dev = lax.rem(s + 1, 64)
    peer = s + 1 - 2 * core
    across = lax.rem(s + 2 * core + 63, 64)

    def y_dev(k):
        return z * 8 + lax.rem(y + k, 4) * 2 + core

    def z_dev(k):
        return lax.rem(z + k, 8) * 8 + y * 2 + core

    def mp_dev(k):
        return lax.rem(m + k, 4)

    barrier = pltpu.get_barrier_semaphore()
    partners = [{"seq": z_dev(k)} for k in (4, 3, 5, 2, 6, 1, 7)]
    for lv in (2, 1, 0):
        for j in range(3):
            for part in range(parts(lv)):
                partners.append({"seq": target(lv, j, part)})
    partners += [{"seq": y_dev(k)} for k in (2, 1, 3)]
    partners += [{"mp": mp_dev(k)} for k in (2, 1, 3)]
    partners += [{"seq": prev_dev}, {"seq": next_dev}]
    for partner in partners:
        pl.semaphore_signal(barrier, inc=1, device_id=partner, device_id_type=MESH)

    def remote(src, dst, send, recv, where):
        return pltpu.make_async_remote_copy(
            src_ref=src, dst_ref=dst, send_sem=send, recv_sem=recv,
            device_id=where, device_id_type=MESH,
        )

    def arrived(ref, sem, spare):
        remote(ref, ref, spare, sem, {"seq": peer}).wait_recv()

    def left(ref, sem, spare):
        remote(ref, ref, sem, spare, {"seq": peer}).wait_send()

    perm = one_hot(natural_token(iota((256, 256), 0)) == iota((256, 256), 1))
    perm_s[...] = perm
    loads[0].wait()
    tok_p = nn(perm, tok_ref[...]).astype(BF16)
    loads[1].wait()
    u0[192:576, :] = nt(wqkv_ref[192:576, :], tok_p)

    def halves(x, lv):
        return x[:, 0:128] + x[:, 128:256] if lv == 0 else x + pltpu.roll(x, 128 >> lv, 1)

    key = unit(u0[192:384, :])
    v = u0[384:576, :]
    kv0[1] = jnp.concatenate([key, v], axis=0).T.astype(BF16)
    pl.semaphore_wait(barrier, len(partners))

    remote(kv0.at[1], kv0.at[2 * core], fs_sem.at[9], fr_sem.at[9], {"seq": peer}).start()
    remote(kv0.at[1], kv0.at[2 - 2 * core], fs_sem.at[10], fr_sem.at[10], {"seq": across}).start()
    for lv in range(3):
        mean = halves(key, lv) * 0.5
        v = halves(v, lv) * ROOT_HALF
        uc[lv, 192:384, :] = mean
        key = unit(mean)
        ownc[lv] = jnp.concatenate([key, v], axis=0).T.astype(BF16)

    mine = (0, core * 64, core * 64 + lax.rem(s // 2, 2) * 32)
    for lv in (2, 1, 0):
        rows = 128 >> lv
        for j in range(2 if lv == 0 else 3):
            i = 3 * lv + back_slot(j)
            for part in range(parts(lv)):
                remote(
                    ownc.at[lv, pl.ds(0, rows)],
                    kvc.at[i, pl.ds(mine[lv], rows)],
                    fs_sem.at[i], fr_sem.at[i], {"seq": target(lv, j, part)},
                ).start()
    def store_q(dst, q_rows, n):
        dst[...] = jnp.zeros(dst.shape, BF16)
        half = (q_rows * 0.5).astype(BF16)
        for h in range(3):
            dst[64 * h : 64 * h + 64, h * n : h * n + n] = half[64 * h : 64 * h + 64]

    loads[2].wait()
    u0[0:192, :] = nt(wqkv_ref[0:192, :], tok_p)
    query = unit(u0[0:192, :])
    store_q(qm0, query, 256)
    q0s[...] = (query * 0.5).astype(BF16)
    for lv in range(3):
        mean = halves(query, lv) * 0.5
        uc[lv, 0:192, :] = mean
        query = unit(mean)
        store_q(qmc.at[lv], query, 128)
        if lv == 0:
            q1s[...] = (query * 0.5).astype(BF16)

    num0[...] = jnp.zeros(num0.shape, F32)
    numc[...] = jnp.zeros(numc.shape, F32)
    den0[...] = jnp.zeros(den0.shape, F32)
    denc[...] = jnp.zeros(denc.shape, F32)
    dq0[...] = jnp.zeros(dq0.shape, F32)
    dqc[...] = jnp.zeros(dqc.shape, F32)
    ra[...] = jnp.zeros(ra.shape, BF16)
    for ref in (qmr0, gmr0, qmr1, gmr1):
        ref[...] = jnp.zeros(ref.shape, BF16)
    pra[0:192, 256:512] = jnp.zeros((192, 256), BF16)
    pra[192:384, 0:256] = jnp.zeros((192, 256), BF16)

    def forward(block, factors, keyst, qm, w_ref, num, den, n):
        count = block.shape[0]
        step = count // len(factors)
        turned = block.astype(F32).T.astype(BF16)
        keyst[...] = turned
        w = jnp.exp(nn(block[:, 0:256], qm[...]))
        w = jnp.concatenate(
            [w[step * k : step * k + step] * factor for k, factor in enumerate(factors)], axis=0
        )
        den[...] += jnp.sum(w.reshape(count // 8, 8, 3 * n), axis=0)
        wb = w.astype(BF16)
        w_ref[...] = wb
        for h in range(3):
            num[64 * h : 64 * h + 64, :] += nn(
                turned[192 + 64 * h : 256 + 64 * h], wb[:, h * n : h * n + n]
            )

    def near_forward(slot, factor):
        forward(kv0[slot], [factor], kvt0.at[slot], qm0, w0.at[slot], num0, den0, 256)

    near, far = 2 - 2 * core, 2 * core
    outside = ((s == 0) & (core == 0)) | ((s == 63) & (core == 1))
    far_keep = jnp.where(outside, jnp.float32(0.0), jnp.float32(1.0))
    one = jnp.float32(1.0)
    near_forward(1, one)

    loads[3].wait()
    loads[4].wait()
    gy_p = nn(perm, gy_ref[...]).astype(BF16)
    dot_s[...] = nt(wout_ref[...], gy_p).astype(BF16)
    for half in range(2):
        index = iota((384, 768), 0)
        twelfth = (index * 5462) >> 16
        rest = half * 12 + (index - 12 * twelfth)
        feature = (twelfth >> 2) * 96 + (twelfth & 3) * 24 + rest
        pick = one_hot(feature == iota((384, 768), 1))
        tg[half, :, 0:256] = nt(pick, tok_p).astype(BF16)
        tg[half, :, 256:512] = nt(pick, gy_p).astype(BF16)
        feature = (twelfth & 7) * 96 + (twelfth >> 3) * 24 + rest
        pick = one_hot(feature == iota((384, 768), 1))
        tg[half, :, 512:768] = nt(pick, tok_p).astype(BF16)
    remote(tg.at[1 - core], ptg, cs_sem.at[0], cr_sem.at[0], {"seq": peer}).start()

    arrived(kv0.at[near], fr_sem.at[9], fs_sem.at[9])
    near_forward(near, one)

    same = one_hot(iota((256, 256), 0) == iota((256, 256), 1))
    for n in range(3):
        cut = slice(256 * n, 256 * n + 256)
        wot[cut, :] = nt(same, wout_ref[:, cut]).astype(BF16)
        wqt[cut, :] = nt(same, wqkv_ref[0:192, cut]).astype(BF16)
        wkvt[cut, :] = nt(same, wqkv_ref[192:576, cut]).astype(BF16)

    half = core * 64
    other = 64 - half
    arrived(kv0.at[far], fr_sem.at[10], fs_sem.at[10])
    near_forward(far, far_keep)
    for i in range(3, 9):
        piece = kvc.at[i, pl.ds(half, 64)]
        arrived(piece, fr_sem.at[i], fs_sem.at[i])
        remote(piece, piece, hs_sem.at[i], hr_sem.at[i], {"seq": peer}).start()
    arrived(kvc.at[0], fr_sem.at[0], fs_sem.at[0])
    arrived(kvc.at[1], fr_sem.at[1], fs_sem.at[1])
    remote(kvc.at[core], kvc.at[2], hs_sem.at[2], hr_sem.at[2], {"seq": peer}).start()

    def to_owners(own0, own1, got0, got1, base):
        remote(own0, got0, qs_sem.at[base], qr_sem.at[base], {"seq": across}).start()
        for j in range(3):
            k = base + 1 + back_slot(j)
            remote(
                own1, got1.at[back_slot(j)], qs_sem.at[k], qr_sem.at[k], {"seq": target(0, j, 0)}
            ).start()

    to_owners(q0s, q1s, q0r, q1r, 0)

    def level_factor(lv, j):
        place = position[lv] + offset(lv, j)
        inside = (place >= 0) & (place < extent[lv])
        return jnp.where(inside, jnp.float32(2 << lv), jnp.float32(0.0))

    def coarse_forward(lv):
        factors = [level_factor(lv, j) for j in range(3)]
        block = kvc[3 * lv : 3 * lv + 3].reshape(384, 384)
        forward(block, factors, kvtc.at[lv], qmc.at[lv], wc.at[lv], numc, denc, 128)

    for lv in (2, 1):
        for i in range(3 * lv, 3 * lv + 3):
            arrived(kvc.at[i, pl.ds(other, 64)], hr_sem.at[i], hs_sem.at[i])
        coarse_forward(lv)
    arrived(kvc.at[2], hr_sem.at[2], hs_sem.at[2])
    coarse_forward(0)

    lane = iota((1, 128), 1)
    gm0[...] = jnp.zeros(gm0.shape, BF16)
    gmc[...] = jnp.zeros(gmc.shape, BF16)
    offsets0, offsets1 = [], []
    for h in range(3):
        rows = slice(64 * h, 64 * h + 64)
        grows = slice(64 * h + 64, 64 * h + 128)
        coarse = jnp.sum(denc[:, 128 * h : 128 * h + 128], axis=0, keepdims=True)
        den = jnp.sum(den0[:, 256 * h : 256 * h + 256], axis=0, keepdims=True)
        inverse = 1.0 / (den + jnp.concatenate([coarse, coarse], axis=1))
        more = numc[rows, :]
        att = ((num0[rows, :] + jnp.concatenate([more, more], axis=1)) * inverse).astype(BF16)
        ra[192 + 64 * h : 256 + 64 * h, 256:512] = att
        att_s[rows, :] = att
        d_att = dot_s[rows, :].astype(F32)
        g = d_att * inverse
        c = jnp.sum(d_att * att.astype(F32), axis=0, keepdims=True) * inverse
        gm0[grows, 256 * h : 256 * h + 256] = g.astype(BF16)
        g0s[rows, :] = g.astype(BF16)
        offsets0.append(c)
        c0[:, 256 * h : 256 * h + 256] = jnp.broadcast_to(c, (8, 256))
        g = g[:, 0:128] + g[:, 128:256]
        c = c[:, 0:128] + c[:, 128:256]
        g1s[rows, :] = g.astype(BF16)
        offsets1.append(c)
        for lv in range(3):
            if lv > 0:
                g = g + pltpu.roll(g, 128 >> lv, 1)
                c = c + pltpu.roll(jnp.broadcast_to(c, (8, 128)), 128 >> lv, 1)[0:1]
            used = lane < (128 >> lv)
            gmc[lv, grows, 128 * h : 128 * h + 128] = jnp.where(used, g, 0.0).astype(BF16)
            cc[lv, :, 128 * h : 128 * h + 128] = jnp.broadcast_to(
                jnp.where(used, c, 0.0), (8, 128)
            )
    for store, offsets in ((g0s, offsets0), (g1s, offsets1)):
        high = [c.astype(BF16).astype(F32) for c in offsets]
        low = [c - h for c, h in zip(offsets, high)]
        rest = jnp.zeros((10, store.shape[1]), F32)
        store[192:208, :] = jnp.concatenate(high + low + [rest], axis=0).astype(BF16)
    to_owners(g0s, g1s, g0r, g1r, 4)
    remote(
        ra.at[pl.ds(192, 192), pl.ds(256, 256)], pra.at[pl.ds(192, 192), pl.ds(256, 256)],
        cs_sem.at[1], cr_sem.at[1], {"seq": peer},
    ).start()

    def key_part(slope, wb, qm, gm):
        dk = nt(slope, qm[...])
        dv = nt(wb, gm[...])
        return jnp.concatenate(
            [dk[:, 0:128], dk[:, 128:256] + dv[:, 0:128], dv[:, 128:256]], axis=1
        )

    def backward(block, keyst, qm, gm, c_rows, w_ref, dq, n, keys=True):
        wb = w_ref[...]
        inner = nn(block[:, 128:384], gm[...])
        slope = (wb.astype(F32) * (inner - c_rows[0:1, :])).astype(BF16)
        for h in range(3):
            dq[64 * h : 64 * h + 64, :] += nn(
                keyst[64 * h : 64 * h + 64, :], slope[:, h * n : h * n + n]
            )
        return key_part(slope, wb, qm, gm) if keys else None

    def coarse_backward(lv, keys=True):
        block = kvc[3 * lv : 3 * lv + 3].reshape(384, 384)
        return backward(
            block, kvtc.at[lv], qmc.at[lv], gmc.at[lv], cc.at[lv], wc.at[lv], dqc.at[lv], 128, keys
        )

    def owner_backward(block, blocks, qm, gm, n):
        c_rows = []
        for b, (q_got, g_got, factor) in enumerate(blocks):
            for h in range(3):
                lanes = slice((3 * b + h) * n, (3 * b + h + 1) * n)
                qm[64 * h : 64 * h + 64, lanes] = q_got[64 * h : 64 * h + 64, :]
                gm[64 * h + 64 : 64 * h + 128, lanes] = g_got[64 * h : 64 * h + 64, :]
            c = g_got[192:208, :].astype(F32)
            c_rows += [c[h : h + 1] + c[h + 3 : h + 4] for h in range(3)]
        w = jnp.exp(nn(block[:, 0:256], qm[...]))
        w = jnp.concatenate(
            [w[:, 3 * n * b : 3 * n * b + 3 * n] * blk[2] for b, blk in enumerate(blocks)], axis=1
        )
        wb = w.astype(BF16)
        inner = nn(block[:, 128:384], gm[...])
        slope = (wb.astype(F32) * (inner - jnp.concatenate(c_rows, axis=1))).astype(BF16)
        return key_part(slope, wb, qm, gm)

    def to_peer(lv):
        ownf[lv - 1] = coarse_backward(lv).reshape(3, 2, 64, 384)
        dsendc[lv - 1] = ownf[lv - 1, :, 1 - core].astype(BF16)
        remote(
            dsendc.at[lv - 1], sibc.at[lv - 1], ss_sem.at[lv], sr_sem.at[lv], {"seq": peer}
        ).start()

    def return_pairs(lv):
        arrived(sibc.at[lv - 1], sr_sem.at[lv], ss_sem.at[lv])
        outc[lv - 1] = (ownf[lv - 1, :, core] + sibc[lv - 1].astype(F32)).astype(BF16)
        rows = 128 >> lv
        into = 0 if lv == 1 else lax.rem(s // 2, 2) * 32
        for j in range(3):
            k = 3 * lv + back_slot(j)
            for part in range(parts(lv)):
                remote(
                    outc.at[lv - 1, j, pl.ds(part * rows, rows)], retc.at[k - 3, pl.ds(into, rows)],
                    bs_sem.at[k], br_sem.at[k], {"seq": target(lv, j, part)},
                ).start()

    def near_backward(slot, keys=True):
        return backward(kv0[slot], kvt0.at[slot], qm0, gm0, c0, w0.at[slot], dq0, 256, keys)

    to_peer(2)
    to_peer(1)
    dsend0[...] = near_backward(near).astype(BF16)
    return_pairs(2)
    return_pairs(1)
    remote(dsend0, ret0, bs_sem.at[9], br_sem.at[9], {"seq": peer}).start()
    down[...] = near_backward(1)
    near_backward(far, False)
    coarse_backward(0, False)

    def spread(grad, lv):
        if lv == 0:
            return jnp.concatenate([grad, grad], axis=1)
        return grad + pltpu.roll(grad, 128 >> lv, 1)

    grad = round_low(dqc[2] * 0.5)
    for lv in (2, 1, 0):
        grad = unit_back(uc[lv, 0:192, :], grad) * 0.5
        base = dqc[lv - 1] if lv > 0 else dq0[...]
        grad = round_low(base * 0.5) + spread(grad, lv)
    dq_t = unit_back(u0[0:192, :], grad).astype(BF16)
    ra[0:192, 0:256] = dq_t
    remote(
        ra.at[pl.ds(0, 192), pl.ds(0, 256)], pra.at[pl.ds(0, 192), pl.ds(0, 256)],
        cs_sem.at[2], cr_sem.at[2], {"seq": peer},
    ).start()

    att_t = att_s[...]
    for j in range(4):
        mixs[j] = nn(wot[192 * j : 192 * j + 192, :], att_t).astype(BF16)
    for k in range(1, 4):
        remote(
            mixs.at[mp_dev(k)], mixr.at[k - 1], ms_sem.at[k - 1], mr_sem.at[k - 1],
            {"mp": mp_dev(k)},
        ).start()
    for j in range(4):
        gtacc[j] = nn(wqt[192 * j : 192 * j + 192, :], dq_t)

    def widen(blocks):
        at = iota((16 * blocks, 12 * blocks), 0)
        here = (at >> 4) * 12 + (at & 15) == iota((16 * blocks, 12 * blocks), 1)
        return one_hot(here & ((at & 15) < 12))

    part_a = (
        gfa, gsa, wsa,
        ((z, 8, z_dev, zra, zs_sem, zr_sem, 0), (y, 4, y_dev, yra, ys_sem, yr_sem, 0)),
    )
    part_b = (
        gfb, gsb, wsb,
        ((y, 4, y_dev, yrb, ys_sem, yr_sem, 3), (z, 8, z_dev, zrb, zs_sem, zr_sem, 7)),
    )
    part_c = (
        gfc, gsc, wsc,
        ((z, 8, z_dev, zrc, zs_sem, zr_sem, 14), (y, 4, y_dev, yrc, ys_sem, yr_sem, 6)),
    )

    def spread_out(src, rows, axis):
        index, count, device, got, send, recv, base = axis
        for k in range(1, count):
            remote(
                src.at[pl.ds(lax.rem(index + k, count) * rows, rows)], got.at[k - 1],
                send.at[base + k - 1], recv.at[base + k - 1], {"seq": device(k)},
            ).start()

    def gathered(own, axis):
        index, count, device, got, send, recv, base = axis
        for k in range(count - 1):
            arrived(got.at[k], recv.at[base + k], send.at[base + k])
            own += got[k].astype(F32)
        return own

    def stage_one(part, total):
        whole, low_s, wide_s, axes = part
        whole[...] = total
        low_s[...] = total.astype(BF16)
        spread_out(low_s, 384 // axes[0][1], axes[0])

    def stage_two(part):
        whole, low_s, wide_s, axes = part
        rows = 384 // axes[0][1]
        total = gathered(whole[pl.ds(axes[0][0] * rows, rows), :], axes[0])
        wide_s[...] = nn(widen(axes[1][1]), total.astype(BF16)).astype(BF16)
        spread_out(wide_s, 16, axes[1])

    def stage_end(part):
        whole, low_s, wide_s, axes = part
        own = wide_s[pl.ds(axes[1][0] * 16, 16), :].astype(F32)
        return gathered(own, axes[1]) * NORM

    def stage_left(part):
        whole, low_s, wide_s, axes = part
        for rows, src, axis in ((384 // axes[0][1], low_s, axes[0]), (16, wide_s, axes[1])):
            index, count, device, got, send, recv, base = axis
            for k in range(count - 1):
                left(src.at[pl.ds(0, rows)], send.at[base + k], recv.at[base + k])

    arrived(ptg, cr_sem.at[0], cs_sem.at[0])
    arrived(pra.at[pl.ds(192, 192), pl.ds(256, 256)], cr_sem.at[1], cs_sem.at[1])
    arrived(pra.at[pl.ds(0, 192), pl.ds(0, 256)], cr_sem.at[2], cs_sem.at[2])
    stage_one(part_a, nt(tg[core, :, 0:512], ra[...]) + nt(ptg[:, 0:512], pra[...]))

    def received(lv):
        if lv == 0:
            for j in range(3):
                arrived(q1r.at[j], qr_sem.at[1 + j], qs_sem.at[1 + j])
                arrived(g1r.at[j], qr_sem.at[5 + j], qs_sem.at[5 + j])
            blocks = [(q1r.at[j], g1r.at[j], level_factor(0, j)) for j in range(3)]
            total = owner_backward(ownc[0], blocks, qmr1, gmr1, 128)
        else:
            total = jnp.zeros((64, 384), F32)
            for i in range(3 * lv, 3 * lv + 3):
                arrived(retc.at[i - 3], br_sem.at[i], bs_sem.at[i])
                total += retc[i - 3].astype(F32)
            if lv == 2:
                total = total[0:32] + total[32:64]
        total = round_low(total)
        if lv > 0:
            rows = 128 >> lv
            total = jnp.concatenate([total, jnp.zeros((128 - rows, 384), F32)], axis=0)
        return total.T

    arrived(q0r, qr_sem.at[0], qs_sem.at[0])
    arrived(g0r, qr_sem.at[4], qs_sem.at[4])
    down[...] += owner_backward(kv0[1], [(q0r, g0r, far_keep)], qmr0, gmr0, 256)
    total = received(2)
    for lv in (2, 1, 0):
        grad_k = unit_back(uc[lv, 192:384, :], total[0:192]) * 0.5
        grad_v = total[192:384] * ROOT_HALF
        if lv > 0:
            base = received(lv - 1)
        else:
            arrived(ret0, br_sem.at[9], bs_sem.at[9])
            base = down[...] + ret0[...].astype(F32)
            base = round_low(base).T
        total = base + jnp.concatenate([spread(grad_k, lv), spread(grad_v, lv)], axis=0)
    dkv = jnp.concatenate([unit_back(u0[192:384, :], total[0:192]), total[192:384]], axis=0)
    dkvt[...] = dkv.astype(BF16)
    remote(dkvt, pdkvt, cs_sem.at[3], cr_sem.at[3], {"seq": peer}).start()

    dkv_t = dkvt[...]
    own_b = nt(tg[core, :, 512:768], dkv_t[0:256])
    own_c = nt(tg[core, :, 0:256], dkv_t[256:384])
    arrived(pdkvt, cr_sem.at[3], cs_sem.at[3])
    stage_one(part_b, own_b + nt(ptg[:, 512:768], pdkvt[0:256, :]))
    stage_one(part_c, own_c + nt(ptg[:, 0:256], pdkvt[256:384, :]))
    for j in range(4):
        gts[j] = (nn(wkvt[192 * j : 192 * j + 192, :], dkv_t) + gtacc[j]).astype(BF16)
    for k in range(1, 4):
        remote(
            gts.at[mp_dev(k)], gtr.at[k - 1], ms_sem.at[2 + k], mr_sem.at[2 + k],
            {"mp": mp_dev(k)},
        ).start()

    def mp_finish(sent, got, base, out):
        total = sent[m].astype(F32)
        for k in range(3):
            arrived(got.at[k], mr_sem.at[base + k], ms_sem.at[base + k])
            total += got[k].astype(F32)
        out[...] = nn(total.astype(BF16), perm_s[...]).astype(BF16)

    mp_finish(mixs, mixr, 0, mixed_ref)
    stage_two(part_b)
    stage_two(part_c)
    stage_two(part_a)
    first = stage_end(part_a)
    go_ref[...] = pltpu.roll(first, 192, 1)[0:12, 0:192]
    gw_ref[:, 0, :] = first[0:12, 0:192]
    mp_finish(gts, gtr, 3, gt_ref)

    for i in range(2):
        left(ownc.at[0], fs_sem.at[i], fr_sem.at[i])
        left(kv0.at[1], fs_sem.at[9 + i], fr_sem.at[9 + i])
    left(dsend0, bs_sem.at[9], br_sem.at[9])
    for base, src0, src1 in ((0, q0s, q1s), (4, g0s, g1s)):
        left(src0, qs_sem.at[base], qr_sem.at[base])
        for k in range(1, 4):
            left(src1, qs_sem.at[base + k], qr_sem.at[base + k])
    left(ownc.at[0], hs_sem.at[2], hr_sem.at[2])
    for lv in (1, 2):
        left(dsendc.at[0], ss_sem.at[lv], sr_sem.at[lv])
    for i in range(3, 9):
        left(outc.at[0, 0], fs_sem.at[i], fr_sem.at[i])
        left(outc.at[0, 0], hs_sem.at[i], hr_sem.at[i])
        left(outc.at[0, 0], bs_sem.at[i], br_sem.at[i])
    left(ptg, cs_sem.at[0], cr_sem.at[0])
    left(ra.at[pl.ds(192, 192), pl.ds(256, 256)], cs_sem.at[1], cr_sem.at[1])
    left(ra.at[pl.ds(0, 192), pl.ds(0, 256)], cs_sem.at[2], cr_sem.at[2])
    left(dkvt, cs_sem.at[3], cr_sem.at[3])
    for i in range(6):
        left(mixs.at[0], ms_sem.at[i], mr_sem.at[i])
    stage_left(part_a)
    stage_left(part_c)
    third = stage_end(part_c)
    second = jnp.concatenate([stage_end(part_b), third], axis=1)
    gw_ref[:, 1, :] = second[0:12, 0:192]
    gw_ref[:, 2, :] = pltpu.roll(second, 192, 1)[0:12, 0:192]
    stage_left(part_b)


def deliver(*refs):
    count = (len(refs) - 1) // 2
    copies = [
        pltpu.make_async_copy(refs[n], refs[count + n], refs[-1].at[n]) for n in range(count)
    ]
    for copy in copies:
        copy.start()
    for copy in copies:
        copy.wait()


def shards(tokens, w_qkv, w_out, grad_y):
    vmem = pl.BlockSpec(memory_space=pltpu.VMEM)
    hbm = pl.BlockSpec(memory_space=pltpu.HBM)
    low = lambda *shape: pltpu.VMEM(shape, BF16)
    wide = lambda *shape: pltpu.VMEM(shape, F32)
    sems = lambda count: pltpu.SemaphoreType.DMA((count,))
    scratch = [
        low(256, 768), low(576, 768), low(192, 768), low(256, 768),
        low(768, 192), low(768, 192), low(768, 384),
        low(256, 256), wide(576, 256), wide(3, 384, 128),
        low(3, 256, 384), low(9, 128, 384), low(3, 128, 384), low(3, 384, 256), low(3, 384, 384),
        low(3, 256, 768), low(3, 384, 384), low(256, 768), low(3, 256, 384),
        low(256, 768), low(3, 256, 384), wide(8, 768), wide(3, 8, 384),
        wide(192, 256), wide(192, 128), wide(8, 768), wide(8, 384), low(192, 256), low(192, 256),
        wide(192, 256), wide(3, 192, 128), wide(256, 384),
        low(256, 384), low(2, 3, 64, 384), low(256, 384), low(6, 64, 384),
        wide(2, 3, 2, 64, 384), low(2, 3, 64, 384), low(2, 3, 64, 384),
        low(192, 256), low(192, 128), low(192, 256), low(3, 192, 128),
        low(208, 256), low(208, 128), low(208, 256), low(3, 208, 128),
        low(256, 768), low(256, 768), low(256, 1152), low(256, 1152),
        low(2, 384, 768), low(384, 768), low(384, 512), low(384, 512), low(384, 256), low(384, 256),
        low(4, 192, 256), low(3, 192, 256), wide(4, 192, 256), low(4, 192, 256), low(3, 192, 256),
        wide(384, 384), low(384, 384), low(64, 384), low(7, 48, 384), low(3, 16, 384),
        wide(384, 256), low(384, 256), low(128, 256), low(3, 96, 256), low(7, 16, 256),
        wide(384, 128), low(384, 128), low(64, 128), low(7, 48, 128), low(3, 16, 128),
        sems(5), sems(11), sems(11), sems(9), sems(9), sems(11), sems(11), sems(3), sems(3),
        sems(8), sems(8), sems(4), sems(4), sems(6), sems(6), sems(9), sems(9), sems(21), sems(21),
    ]
    shapes = (
        jax.ShapeDtypeStruct((192, 256), BF16),
        jax.ShapeDtypeStruct((192, 256), BF16),
        jax.ShapeDtypeStruct((12, 3, 192), F32),
        jax.ShapeDtypeStruct((12, 192), F32),
    )
    results = pl.pallas_call(
        kernel,
        out_shape=shapes,
        in_specs=[hbm] * 4,
        out_specs=(vmem,) * 4,
        scratch_shapes=scratch,
        compiler_params=pltpu.CompilerParams(
            collective_id=0, has_side_effects=True, vmem_limit_bytes=56098816
        ),
        cost_estimate=pl.CostEstimate(
            flops=2_000_000_000, bytes_accessed=4_000_000, transcendentals=1_000_000
        ),
    )(
        tokens.reshape(256, 768), w_qkv.reshape(576, 768), w_out, grad_y.reshape(256, 768)
    )
    mixed, grad_tokens, grad_wqkv, grad_wout = pl.pallas_call(
        deliver,
        out_shape=shapes,
        in_specs=[vmem] * 4,
        out_specs=(hbm,) * 4,
        scratch_shapes=[sems(4)],
        compiler_params=pltpu.CompilerParams(vmem_limit_bytes=1024 * 1024),
    )(*results)
    return (mixed.T[None], grad_tokens.T[None], grad_wqkv, grad_wout)


def solution(mesh):
    in_specs = (P(None, "seq", None), P(None, "mp", None), P("mp", None), P(None, "seq", None))
    out_specs = (P(None, "seq", "mp"), P(None, "seq", "mp"), P("seq", None, "mp"), P("seq", "mp"))
    return jax.shard_map(shards, mesh=mesh, in_specs=in_specs, out_specs=out_specs, check_vma=False)
```

```python
import jax
import jax.numpy as jnp
from jax import lax
from jax.experimental import pallas as pl
from jax.experimental.pallas import tpu as pltpu
from jax.sharding import PartitionSpec as P

F32 = jnp.float32
BF16 = jnp.bfloat16
MESH = pl.DeviceIdType.MESH
EPS = 1e-06
ROOT_HALF = 0.7071067811865476
NORM = 1.0 / 128.0


def nn(a, b):
    return jnp.dot(a, b, preferred_element_type=F32)


def nt(a, b):
    return lax.dot_general(a, b, (((1,), (1,)), ((), ())), preferred_element_type=F32)


def unit_parts(x):
    heads = x.reshape(x.shape[0] // 64, 64, x.shape[1])
    scale = lax.rsqrt(jnp.mean(heads * heads, axis=1, keepdims=True) + EPS)
    return heads * scale, scale


def unit(x):
    return unit_parts(x)[0].reshape(x.shape)


def unit_back(x, grad):
    y, scale = unit_parts(x)
    dy = grad.reshape(y.shape)
    return (scale * (dy - y * jnp.mean(y * dy, axis=1, keepdims=True))).reshape(x.shape)


def round_low(x):
    return x.astype(BF16).astype(F32)


def iota(shape, dim):
    return lax.broadcasted_iota(jnp.int32, shape, dim)


def one_hot(cond):
    return jnp.where(cond, 1.0, 0.0).astype(BF16)


def natural_token(row):
    high = row >> 5
    return (row & 31) * 8 + (((high & 1) << 2) | (high & 2) | ((high >> 2) & 1))


def kernel(
    tok_hbm, wqkv_hbm, wout_hbm, gy_hbm,
    mixed_ref, gt_ref, gw_ref, go_ref,
    tok_ref, wqkv_ref, wout_ref, gy_ref, wot, wqt, wkvt,
    perm_s, u0, uc, kv0, kvc, ownc, kvt0, kvtc, w0, wc, qm0, qmc, gm0, gmc, c0, cc,
    num0, numc, den0, denc, dot_s, att_s, dq0, dqc, down, dsend0, dsendc, ret0, retc,
    ownf, sibc, outc,
    q0s, q1s, q0r, q1r, g0s, g1s, g0r, g1r, qmr0, gmr0, qmr1, gmr1,
    tg, ptg, ra, pra, dkvt, pdkvt, mixs, mixr, gtacc, gts, gtr,
    gfa, gsa, wsa, zra, yra, gfb, gsb, wsb, yrb, zrb, gfc, gsc, wsc, zrc, yrc,
    in_sem, fs_sem, fr_sem, hs_sem, hr_sem, bs_sem, br_sem, ss_sem, sr_sem,
    qs_sem, qr_sem, cs_sem, cr_sem, ms_sem, mr_sem, ys_sem, yr_sem, zs_sem, zr_sem,
):
    loads = [
        pltpu.make_async_copy(src, dst, in_sem.at[n])
        for n, (src, dst) in enumerate((
            (tok_hbm, tok_ref),
            (wqkv_hbm.at[pl.ds(192, 384)], wqkv_ref.at[pl.ds(192, 384)]),
            (wqkv_hbm.at[pl.ds(0, 192)], wqkv_ref.at[pl.ds(0, 192)]),
            (gy_hbm, gy_ref),
            (wout_hbm, wout_ref),
        ))
    ]
    for load in loads:
        load.start()

    s = lax.axis_index("seq")
    m = lax.axis_index("mp")
    core = lax.rem(s, 2)
    y = lax.rem(s // 2, 4)
    z = s // 8
    position = (s, s // 2, s // 4)
    extent = (64, 32, 16)
    skip = [3 - 6 * lax.rem(position[lv], 2) for lv in range(3)]

    def offset(lv, j):
        return (-2, 2, skip[lv])[j]

    def target(lv, j, part):
        block = lax.rem(position[lv] + offset(lv, j) + extent[lv], extent[lv])
        return block if lv == 0 else block * (1 << lv) + 2 * part + core

    def parts(lv):
        return 2 if lv == 2 else 1

    def back_slot(j):
        return (1, 0, 2)[j]

    prev_dev = lax.rem(s + 63, 64)
    next_dev = lax.rem(s + 1, 64)
    peer = s + 1 - 2 * core
    across = lax.rem(s + 2 * core + 63, 64)

    def y_dev(k):
        return z * 8 + lax.rem(y + k, 4) * 2 + core

    def z_dev(k):
        return lax.rem(z + k, 8) * 8 + y * 2 + core

    def mp_dev(k):
        return lax.rem(m + k, 4)

    barrier = pltpu.get_barrier_semaphore()
    partners = [{"seq": z_dev(k)} for k in (4, 3, 5, 2, 6, 1, 7)]
    for lv in (2, 1, 0):
        for j in range(3):
            for part in range(parts(lv)):
                partners.append({"seq": target(lv, j, part)})
    partners += [{"seq": y_dev(k)} for k in (2, 1, 3)]
    partners += [{"mp": mp_dev(k)} for k in (2, 1, 3)]
    partners += [{"seq": prev_dev}, {"seq": next_dev}]
    for partner in partners:
        pl.semaphore_signal(barrier, inc=1, device_id=partner, device_id_type=MESH)

    def remote(src, dst, send, recv, where):
        return pltpu.make_async_remote_copy(
            src_ref=src, dst_ref=dst, send_sem=send, recv_sem=recv,
            device_id=where, device_id_type=MESH,
        )

    def arrived(ref, sem, spare):
        remote(ref, ref, spare, sem, {"seq": peer}).wait_recv()

    def left(ref, sem, spare):
        remote(ref, ref, sem, spare, {"seq": peer}).wait_send()

    perm = one_hot(natural_token(iota((256, 256), 0)) == iota((256, 256), 1))
    perm_s[...] = perm
    loads[0].wait()
    tok_p = nn(perm, tok_ref[...]).astype(BF16)
    loads[1].wait()
    u0[192:576, :] = nt(wqkv_ref[192:576, :], tok_p)

    def halves(x, lv):
        return x[:, 0:128] + x[:, 128:256] if lv == 0 else x + pltpu.roll(x, 128 >> lv, 1)

    key = unit(u0[192:384, :])
    v = u0[384:576, :]
    kv0[1] = jnp.concatenate([key, v], axis=0).T.astype(BF16)
    pl.semaphore_wait(barrier, len(partners))

    remote(kv0.at[1], kv0.at[2 * core], fs_sem.at[9], fr_sem.at[9], {"seq": peer}).start()
    remote(kv0.at[1], kv0.at[2 - 2 * core], fs_sem.at[10], fr_sem.at[10], {"seq": across}).start()
    for lv in range(3):
        mean = halves(key, lv) * 0.5
        v = halves(v, lv) * ROOT_HALF
        uc[lv, 192:384, :] = mean
        key = unit(mean)
        ownc[lv] = jnp.concatenate([key, v], axis=0).T.astype(BF16)

    mine = (0, core * 64, core * 64 + lax.rem(s // 2, 2) * 32)
    for lv in (2, 1, 0):
        rows = 128 >> lv
        for j in range(2 if lv == 0 else 3):
            i = 3 * lv + back_slot(j)
            for part in range(parts(lv)):
                remote(
                    ownc.at[lv, pl.ds(0, rows)],
                    kvc.at[i, pl.ds(mine[lv], rows)],
                    fs_sem.at[i], fr_sem.at[i], {"seq": target(lv, j, part)},
                ).start()
    def store_q(dst, q_rows, n):
        dst[...] = jnp.zeros(dst.shape, BF16)
        half = (q_rows * 0.5).astype(BF16)
        for h in range(3):
            dst[64 * h : 64 * h + 64, h * n : h * n + n] = half[64 * h : 64 * h + 64]

    loads[2].wait()
    u0[0:192, :] = nt(wqkv_ref[0:192, :], tok_p)
    query = unit(u0[0:192, :])
    store_q(qm0, query, 256)
    q0s[...] = (query * 0.5).astype(BF16)
    for lv in range(3):
        mean = halves(query, lv) * 0.5
        uc[lv, 0:192, :] = mean
        query = unit(mean)
        store_q(qmc.at[lv], query, 128)
        if lv == 0:
            q1s[...] = (query * 0.5).astype(BF16)

    num0[...] = jnp.zeros(num0.shape, F32)
    numc[...] = jnp.zeros(numc.shape, F32)
    den0[...] = jnp.zeros(den0.shape, F32)
    denc[...] = jnp.zeros(denc.shape, F32)
    dq0[...] = jnp.zeros(dq0.shape, F32)
    dqc[...] = jnp.zeros(dqc.shape, F32)
    ra[...] = jnp.zeros(ra.shape, BF16)
    for ref in (qmr0, gmr0, qmr1, gmr1):
        ref[...] = jnp.zeros(ref.shape, BF16)
    pra[0:192, 256:512] = jnp.zeros((192, 256), BF16)
    pra[192:384, 0:256] = jnp.zeros((192, 256), BF16)

    def forward(block, factors, keyst, qm, w_ref, num, den, n):
        count = block.shape[0]
        step = count // len(factors)
        turned = block.astype(F32).T.astype(BF16)
        keyst[...] = turned
        w = jnp.exp(nn(block[:, 0:256], qm[...]))
        w = jnp.concatenate(
            [w[step * k : step * k + step] * factor for k, factor in enumerate(factors)], axis=0
        )
        den[...] += jnp.sum(w.reshape(count // 8, 8, 3 * n), axis=0)
        wb = w.astype(BF16)
        w_ref[...] = wb
        for h in range(3):
            num[64 * h : 64 * h + 64, :] += nn(
                turned[192 + 64 * h : 256 + 64 * h], wb[:, h * n : h * n + n]
            )

    def near_forward(slot, factor):
        forward(kv0[slot], [factor], kvt0.at[slot], qm0, w0.at[slot], num0, den0, 256)

    near, far = 2 - 2 * core, 2 * core
    outside = ((s == 0) & (core == 0)) | ((s == 63) & (core == 1))
    far_keep = jnp.where(outside, jnp.float32(0.0), jnp.float32(1.0))
    one = jnp.float32(1.0)
    near_forward(1, one)

    loads[3].wait()
    loads[4].wait()
    gy_p = nn(perm, gy_ref[...]).astype(BF16)
    dot_s[...] = nt(wout_ref[...], gy_p).astype(BF16)
    for half in range(2):
        index = iota((384, 768), 0)
        twelfth = (index * 5462) >> 16
        rest = half * 12 + (index - 12 * twelfth)
        feature = (twelfth >> 2) * 96 + (twelfth & 3) * 24 + rest
        pick = one_hot(feature == iota((384, 768), 1))
        tg[half, :, 0:256] = nt(pick, tok_p).astype(BF16)
        tg[half, :, 256:512] = nt(pick, gy_p).astype(BF16)
        feature = (twelfth & 7) * 96 + (twelfth >> 3) * 24 + rest
        pick = one_hot(feature == iota((384, 768), 1))
        tg[half, :, 512:768] = nt(pick, tok_p).astype(BF16)
    remote(tg.at[1 - core], ptg, cs_sem.at[0], cr_sem.at[0], {"seq": peer}).start()

    arrived(kv0.at[near], fr_sem.at[9], fs_sem.at[9])
    near_forward(near, one)

    same = one_hot(iota((256, 256), 0) == iota((256, 256), 1))
    for n in range(3):
        cut = slice(256 * n, 256 * n + 256)
        wot[cut, :] = nt(same, wout_ref[:, cut]).astype(BF16)
        wqt[cut, :] = nt(same, wqkv_ref[0:192, cut]).astype(BF16)
        wkvt[cut, :] = nt(same, wqkv_ref[192:576, cut]).astype(BF16)

    half = core * 64
    other = 64 - half
    arrived(kv0.at[far], fr_sem.at[10], fs_sem.at[10])
    near_forward(far, far_keep)
    for i in range(3, 9):
        piece = kvc.at[i, pl.ds(half, 64)]
        arrived(piece, fr_sem.at[i], fs_sem.at[i])
        remote(piece, piece, hs_sem.at[i], hr_sem.at[i], {"seq": peer}).start()
    arrived(kvc.at[0], fr_sem.at[0], fs_sem.at[0])
    arrived(kvc.at[1], fr_sem.at[1], fs_sem.at[1])
    remote(kvc.at[core], kvc.at[2], hs_sem.at[2], hr_sem.at[2], {"seq": peer}).start()

    def to_owners(own0, own1, got0, got1, base):
        remote(own0, got0, qs_sem.at[base], qr_sem.at[base], {"seq": across}).start()
        for j in range(3):
            k = base + 1 + back_slot(j)
            remote(
                own1, got1.at[back_slot(j)], qs_sem.at[k], qr_sem.at[k], {"seq": target(0, j, 0)}
            ).start()

    to_owners(q0s, q1s, q0r, q1r, 0)

    def level_factor(lv, j):
        place = position[lv] + offset(lv, j)
        inside = (place >= 0) & (place < extent[lv])
        return jnp.where(inside, jnp.float32(2 << lv), jnp.float32(0.0))

    def coarse_forward(lv):
        factors = [level_factor(lv, j) for j in range(3)]
        block = kvc[3 * lv : 3 * lv + 3].reshape(384, 384)
        forward(block, factors, kvtc.at[lv], qmc.at[lv], wc.at[lv], numc, denc, 128)

    for lv in (2, 1):
        for i in range(3 * lv, 3 * lv + 3):
            arrived(kvc.at[i, pl.ds(other, 64)], hr_sem.at[i], hs_sem.at[i])
        coarse_forward(lv)
    arrived(kvc.at[2], hr_sem.at[2], hs_sem.at[2])
    coarse_forward(0)

    lane = iota((1, 128), 1)
    gm0[...] = jnp.zeros(gm0.shape, BF16)
    gmc[...] = jnp.zeros(gmc.shape, BF16)
    offsets0, offsets1 = [], []
    for h in range(3):
        rows = slice(64 * h, 64 * h + 64)
        grows = slice(64 * h + 64, 64 * h + 128)
        coarse = jnp.sum(denc[:, 128 * h : 128 * h + 128], axis=0, keepdims=True)
        den = jnp.sum(den0[:, 256 * h : 256 * h + 256], axis=0, keepdims=True)
        inverse = 1.0 / (den + jnp.concatenate([coarse, coarse], axis=1))
        more = numc[rows, :]
        att = ((num0[rows, :] + jnp.concatenate([more, more], axis=1)) * inverse).astype(BF16)
        ra[192 + 64 * h : 256 + 64 * h, 256:512] = att
        att_s[rows, :] = att
        d_att = dot_s[rows, :].astype(F32)
        g = d_att * inverse
        c = jnp.sum(d_att * att.astype(F32), axis=0, keepdims=True) * inverse
        gm0[grows, 256 * h : 256 * h + 256] = g.astype(BF16)
        g0s[rows, :] = g.astype(BF16)
        offsets0.append(c)
        c0[:, 256 * h : 256 * h + 256] = jnp.broadcast_to(c, (8, 256))
        g = g[:, 0:128] + g[:, 128:256]
        c = c[:, 0:128] + c[:, 128:256]
        g1s[rows, :] = g.astype(BF16)
        offsets1.append(c)
        for lv in range(3):
            if lv > 0:
                g = g + pltpu.roll(g, 128 >> lv, 1)
                c = c + pltpu.roll(jnp.broadcast_to(c, (8, 128)), 128 >> lv, 1)[0:1]
            used = lane < (128 >> lv)
            gmc[lv, grows, 128 * h : 128 * h + 128] = jnp.where(used, g, 0.0).astype(BF16)
            cc[lv, :, 128 * h : 128 * h + 128] = jnp.broadcast_to(
                jnp.where(used, c, 0.0), (8, 128)
            )
    for store, offsets in ((g0s, offsets0), (g1s, offsets1)):
        high = [c.astype(BF16).astype(F32) for c in offsets]
        low = [c - h for c, h in zip(offsets, high)]
        rest = jnp.zeros((10, store.shape[1]), F32)
        store[192:208, :] = jnp.concatenate(high + low + [rest], axis=0).astype(BF16)
    to_owners(g0s, g1s, g0r, g1r, 4)
    remote(
        ra.at[pl.ds(192, 192), pl.ds(256, 256)], pra.at[pl.ds(192, 192), pl.ds(256, 256)],
        cs_sem.at[1], cr_sem.at[1], {"seq": peer},
    ).start()

    def key_part(slope, wb, qm, gm):
        dk = nt(slope, qm[...])
        dv = nt(wb, gm[...])
        return jnp.concatenate(
            [dk[:, 0:128], dk[:, 128:256] + dv[:, 0:128], dv[:, 128:256]], axis=1
        )

    def backward(block, keyst, qm, gm, c_rows, w_ref, dq, n, keys=True):
        wb = w_ref[...]
        inner = nn(block[:, 128:384], gm[...])
        slope = (wb.astype(F32) * (inner - c_rows[0:1, :])).astype(BF16)
        for h in range(3):
            dq[64 * h : 64 * h + 64, :] += nn(
                keyst[64 * h : 64 * h + 64, :], slope[:, h * n : h * n + n]
            )
        return key_part(slope, wb, qm, gm) if keys else None

    def coarse_backward(lv, keys=True):
        block = kvc[3 * lv : 3 * lv + 3].reshape(384, 384)
        return backward(
            block, kvtc.at[lv], qmc.at[lv], gmc.at[lv], cc.at[lv], wc.at[lv], dqc.at[lv], 128, keys
        )

    def owner_backward(block, blocks, qm, gm, n):
        c_rows = []
        for b, (q_got, g_got, factor) in enumerate(blocks):
            for h in range(3):
                lanes = slice((3 * b + h) * n, (3 * b + h + 1) * n)
                qm[64 * h : 64 * h + 64, lanes] = q_got[64 * h : 64 * h + 64, :]
                gm[64 * h + 64 : 64 * h + 128, lanes] = g_got[64 * h : 64 * h + 64, :]
            c = g_got[192:208, :].astype(F32)
            c_rows += [c[h : h + 1] + c[h + 3 : h + 4] for h in range(3)]
        w = jnp.exp(nn(block[:, 0:256], qm[...]))
        w = jnp.concatenate(
            [w[:, 3 * n * b : 3 * n * b + 3 * n] * blk[2] for b, blk in enumerate(blocks)], axis=1
        )
        wb = w.astype(BF16)
        inner = nn(block[:, 128:384], gm[...])
        slope = (wb.astype(F32) * (inner - jnp.concatenate(c_rows, axis=1))).astype(BF16)
        return key_part(slope, wb, qm, gm)

    def to_peer(lv):
        ownf[lv - 1] = coarse_backward(lv).reshape(3, 2, 64, 384)
        dsendc[lv - 1] = ownf[lv - 1, :, 1 - core].astype(BF16)
        remote(
            dsendc.at[lv - 1], sibc.at[lv - 1], ss_sem.at[lv], sr_sem.at[lv], {"seq": peer}
        ).start()

    def return_pairs(lv):
        arrived(sibc.at[lv - 1], sr_sem.at[lv], ss_sem.at[lv])
        outc[lv - 1] = (ownf[lv - 1, :, core] + sibc[lv - 1].astype(F32)).astype(BF16)
        rows = 128 >> lv
        into = 0 if lv == 1 else lax.rem(s // 2, 2) * 32
        for j in range(3):
            k = 3 * lv + back_slot(j)
            for part in range(parts(lv)):
                remote(
                    outc.at[lv - 1, j, pl.ds(part * rows, rows)], retc.at[k - 3, pl.ds(into, rows)],
                    bs_sem.at[k], br_sem.at[k], {"seq": target(lv, j, part)},
                ).start()

    def near_backward(slot, keys=True):
        return backward(kv0[slot], kvt0.at[slot], qm0, gm0, c0, w0.at[slot], dq0, 256, keys)

    to_peer(2)
    to_peer(1)
    dsend0[...] = near_backward(near).astype(BF16)
    return_pairs(2)
    return_pairs(1)
    remote(dsend0, ret0, bs_sem.at[9], br_sem.at[9], {"seq": peer}).start()
    down[...] = near_backward(1)
    near_backward(far, False)
    coarse_backward(0, False)

    def spread(grad, lv):
        if lv == 0:
            return jnp.concatenate([grad, grad], axis=1)
        return grad + pltpu.roll(grad, 128 >> lv, 1)

    grad = round_low(dqc[2] * 0.5)
    for lv in (2, 1, 0):
        grad = unit_back(uc[lv, 0:192, :], grad) * 0.5
        base = dqc[lv - 1] if lv > 0 else dq0[...]
        grad = round_low(base * 0.5) + spread(grad, lv)
    dq_t = unit_back(u0[0:192, :], grad).astype(BF16)
    ra[0:192, 0:256] = dq_t
    remote(
        ra.at[pl.ds(0, 192), pl.ds(0, 256)], pra.at[pl.ds(0, 192), pl.ds(0, 256)],
        cs_sem.at[2], cr_sem.at[2], {"seq": peer},
    ).start()

    arrived(q0r, qr_sem.at[0], qs_sem.at[0])
    arrived(g0r, qr_sem.at[4], qs_sem.at[4])
    down[...] += owner_backward(kv0[1], [(q0r, g0r, far_keep)], qmr0, gmr0, 256)
    att_t = att_s[...]
    for j in range(4):
        mixs[j] = nn(wot[192 * j : 192 * j + 192, :], att_t).astype(BF16)
    for k in range(1, 4):
        remote(
            mixs.at[mp_dev(k)], mixr.at[k - 1], ms_sem.at[k - 1], mr_sem.at[k - 1],
            {"mp": mp_dev(k)},
        ).start()

    def widen(blocks):
        at = iota((16 * blocks, 12 * blocks), 0)
        here = (at >> 4) * 12 + (at & 15) == iota((16 * blocks, 12 * blocks), 1)
        return one_hot(here & ((at & 15) < 12))

    part_a = (
        gfa, gsa, wsa,
        ((z, 8, z_dev, zra, zs_sem, zr_sem, 0), (y, 4, y_dev, yra, ys_sem, yr_sem, 0)),
    )
    part_b = (
        gfb, gsb, wsb,
        ((y, 4, y_dev, yrb, ys_sem, yr_sem, 3), (z, 8, z_dev, zrb, zs_sem, zr_sem, 7)),
    )
    part_c = (
        gfc, gsc, wsc,
        ((z, 8, z_dev, zrc, zs_sem, zr_sem, 14), (y, 4, y_dev, yrc, ys_sem, yr_sem, 6)),
    )

    def spread_out(src, rows, axis):
        index, count, device, got, send, recv, base = axis
        for k in range(1, count):
            remote(
                src.at[pl.ds(lax.rem(index + k, count) * rows, rows)], got.at[k - 1],
                send.at[base + k - 1], recv.at[base + k - 1], {"seq": device(k)},
            ).start()

    def gathered(own, axis):
        index, count, device, got, send, recv, base = axis
        for k in range(count - 1):
            arrived(got.at[k], recv.at[base + k], send.at[base + k])
            own += got[k].astype(F32)
        return own

    def stage_one(part, total):
        whole, low_s, wide_s, axes = part
        whole[...] = total
        low_s[...] = total.astype(BF16)
        spread_out(low_s, 384 // axes[0][1], axes[0])

    def stage_two(part):
        whole, low_s, wide_s, axes = part
        rows = 384 // axes[0][1]
        total = gathered(whole[pl.ds(axes[0][0] * rows, rows), :], axes[0])
        wide_s[...] = nn(widen(axes[1][1]), total.astype(BF16)).astype(BF16)
        spread_out(wide_s, 16, axes[1])

    def stage_end(part):
        whole, low_s, wide_s, axes = part
        own = wide_s[pl.ds(axes[1][0] * 16, 16), :].astype(F32)
        return gathered(own, axes[1]) * NORM

    def stage_left(part):
        whole, low_s, wide_s, axes = part
        for rows, src, axis in ((384 // axes[0][1], low_s, axes[0]), (16, wide_s, axes[1])):
            index, count, device, got, send, recv, base = axis
            for k in range(count - 1):
                left(src.at[pl.ds(0, rows)], send.at[base + k], recv.at[base + k])

    arrived(ptg, cr_sem.at[0], cs_sem.at[0])
    arrived(pra.at[pl.ds(192, 192), pl.ds(256, 256)], cr_sem.at[1], cs_sem.at[1])
    arrived(pra.at[pl.ds(0, 192), pl.ds(0, 256)], cr_sem.at[2], cs_sem.at[2])
    stage_one(part_a, nt(tg[core, :, 0:512], ra[...]) + nt(ptg[:, 0:512], pra[...]))

    def received(lv):
        if lv == 0:
            for j in range(3):
                arrived(q1r.at[j], qr_sem.at[1 + j], qs_sem.at[1 + j])
                arrived(g1r.at[j], qr_sem.at[5 + j], qs_sem.at[5 + j])
            blocks = [(q1r.at[j], g1r.at[j], level_factor(0, j)) for j in range(3)]
            total = owner_backward(ownc[0], blocks, qmr1, gmr1, 128)
        else:
            total = jnp.zeros((64, 384), F32)
            for i in range(3 * lv, 3 * lv + 3):
                arrived(retc.at[i - 3], br_sem.at[i], bs_sem.at[i])
                total += retc[i - 3].astype(F32)
            if lv == 2:
                total = total[0:32] + total[32:64]
        total = round_low(total)
        if lv > 0:
            rows = 128 >> lv
            total = jnp.concatenate([total, jnp.zeros((128 - rows, 384), F32)], axis=0)
        return total.T

    total = received(2)
    for lv in (2, 1, 0):
        grad_k = unit_back(uc[lv, 192:384, :], total[0:192]) * 0.5
        grad_v = total[192:384] * ROOT_HALF
        if lv > 0:
            base = received(lv - 1)
        else:
            arrived(ret0, br_sem.at[9], bs_sem.at[9])
            base = down[...] + ret0[...].astype(F32)
            base = round_low(base).T
        total = base + jnp.concatenate([spread(grad_k, lv), spread(grad_v, lv)], axis=0)
    dkv = jnp.concatenate([unit_back(u0[192:384, :], total[0:192]), total[192:384]], axis=0)
    dkvt[...] = dkv.astype(BF16)
    remote(dkvt, pdkvt, cs_sem.at[3], cr_sem.at[3], {"seq": peer}).start()

    dkv_t = dkvt[...]
    own_b = nt(tg[core, :, 512:768], dkv_t[0:256])
    own_c = nt(tg[core, :, 0:256], dkv_t[256:384])
    arrived(pdkvt, cr_sem.at[3], cs_sem.at[3])
    stage_one(part_b, own_b + nt(ptg[:, 512:768], pdkvt[0:256, :]))
    stage_one(part_c, own_c + nt(ptg[:, 0:256], pdkvt[256:384, :]))
    for j in range(4):
        gtacc[j] = nn(wqt[192 * j : 192 * j + 192, :], dq_t)
    for j in range(4):
        gts[j] = (nn(wkvt[192 * j : 192 * j + 192, :], dkv_t) + gtacc[j]).astype(BF16)
    for k in range(1, 4):
        remote(
            gts.at[mp_dev(k)], gtr.at[k - 1], ms_sem.at[2 + k], mr_sem.at[2 + k],
            {"mp": mp_dev(k)},
        ).start()

    def mp_finish(sent, got, base, out):
        total = sent[m].astype(F32)
        for k in range(3):
            arrived(got.at[k], mr_sem.at[base + k], ms_sem.at[base + k])
            total += got[k].astype(F32)
        out[...] = nn(total.astype(BF16), perm_s[...]).astype(BF16)

    mp_finish(mixs, mixr, 0, mixed_ref)
    stage_two(part_b)
    stage_two(part_c)
    stage_two(part_a)
    first = stage_end(part_a)
    go_ref[...] = pltpu.roll(first, 192, 1)[0:12, 0:192]
    gw_ref[:, 0, :] = first[0:12, 0:192]
    mp_finish(gts, gtr, 3, gt_ref)

    for i in range(2):
        left(ownc.at[0], fs_sem.at[i], fr_sem.at[i])
        left(kv0.at[1], fs_sem.at[9 + i], fr_sem.at[9 + i])
    left(dsend0, bs_sem.at[9], br_sem.at[9])
    for base, src0, src1 in ((0, q0s, q1s), (4, g0s, g1s)):
        left(src0, qs_sem.at[base], qr_sem.at[base])
        for k in range(1, 4):
            left(src1, qs_sem.at[base + k], qr_sem.at[base + k])
    left(ownc.at[0], hs_sem.at[2], hr_sem.at[2])
    for lv in (1, 2):
        left(dsendc.at[0], ss_sem.at[lv], sr_sem.at[lv])
    for i in range(3, 9):
        left(outc.at[0, 0], fs_sem.at[i], fr_sem.at[i])
        left(outc.at[0, 0], hs_sem.at[i], hr_sem.at[i])
        left(outc.at[0, 0], bs_sem.at[i], br_sem.at[i])
    left(ptg, cs_sem.at[0], cr_sem.at[0])
    left(ra.at[pl.ds(192, 192), pl.ds(256, 256)], cs_sem.at[1], cr_sem.at[1])
    left(ra.at[pl.ds(0, 192), pl.ds(0, 256)], cs_sem.at[2], cr_sem.at[2])
    left(dkvt, cs_sem.at[3], cr_sem.at[3])
    for i in range(6):
        left(mixs.at[0], ms_sem.at[i], mr_sem.at[i])
    stage_left(part_a)
    stage_left(part_c)
    third = stage_end(part_c)
    second = jnp.concatenate([stage_end(part_b), third], axis=1)
    gw_ref[:, 1, :] = second[0:12, 0:192]
    gw_ref[:, 2, :] = pltpu.roll(second, 192, 1)[0:12, 0:192]
    stage_left(part_b)


def deliver(*refs):
    count = (len(refs) - 1) // 2
    copies = [
        pltpu.make_async_copy(refs[n], refs[count + n], refs[-1].at[n]) for n in range(count)
    ]
    for copy in copies:
        copy.start()
    for copy in copies:
        copy.wait()


def shards(tokens, w_qkv, w_out, grad_y):
    vmem = pl.BlockSpec(memory_space=pltpu.VMEM)
    hbm = pl.BlockSpec(memory_space=pltpu.HBM)
    low = lambda *shape: pltpu.VMEM(shape, BF16)
    wide = lambda *shape: pltpu.VMEM(shape, F32)
    sems = lambda count: pltpu.SemaphoreType.DMA((count,))
    scratch = [
        low(256, 768), low(576, 768), low(192, 768), low(256, 768),
        low(768, 192), low(768, 192), low(768, 384),
        low(256, 256), wide(576, 256), wide(3, 384, 128),
        low(3, 256, 384), low(9, 128, 384), low(3, 128, 384), low(3, 384, 256), low(3, 384, 384),
        low(3, 256, 768), low(3, 384, 384), low(256, 768), low(3, 256, 384),
        low(256, 768), low(3, 256, 384), wide(8, 768), wide(3, 8, 384),
        wide(192, 256), wide(192, 128), wide(8, 768), wide(8, 384), low(192, 256), low(192, 256),
        wide(192, 256), wide(3, 192, 128), wide(256, 384),
        low(256, 384), low(2, 3, 64, 384), low(256, 384), low(6, 64, 384),
        wide(2, 3, 2, 64, 384), low(2, 3, 64, 384), low(2, 3, 64, 384),
        low(192, 256), low(192, 128), low(192, 256), low(3, 192, 128),
        low(208, 256), low(208, 128), low(208, 256), low(3, 208, 128),
        low(256, 768), low(256, 768), low(256, 1152), low(256, 1152),
        low(2, 384, 768), low(384, 768), low(384, 512), low(384, 512), low(384, 256), low(384, 256),
        low(4, 192, 256), low(3, 192, 256), wide(4, 192, 256), low(4, 192, 256), low(3, 192, 256),
        wide(384, 384), low(384, 384), low(64, 384), low(7, 48, 384), low(3, 16, 384),
        wide(384, 256), low(384, 256), low(128, 256), low(3, 96, 256), low(7, 16, 256),
        wide(384, 128), low(384, 128), low(64, 128), low(7, 48, 128), low(3, 16, 128),
        sems(5), sems(11), sems(11), sems(9), sems(9), sems(11), sems(11), sems(3), sems(3),
        sems(8), sems(8), sems(4), sems(4), sems(6), sems(6), sems(9), sems(9), sems(21), sems(21),
    ]
    shapes = (
        jax.ShapeDtypeStruct((192, 256), BF16),
        jax.ShapeDtypeStruct((192, 256), BF16),
        jax.ShapeDtypeStruct((12, 3, 192), F32),
        jax.ShapeDtypeStruct((12, 192), F32),
    )
    results = pl.pallas_call(
        kernel,
        out_shape=shapes,
        in_specs=[hbm] * 4,
        out_specs=(vmem,) * 4,
        scratch_shapes=scratch,
        compiler_params=pltpu.CompilerParams(
            collective_id=0, has_side_effects=True, vmem_limit_bytes=56098816
        ),
        cost_estimate=pl.CostEstimate(
            flops=2_000_000_000, bytes_accessed=4_000_000, transcendentals=1_000_000
        ),
    )(
        tokens.reshape(256, 768), w_qkv.reshape(576, 768), w_out, grad_y.reshape(256, 768)
    )
    mixed, grad_tokens, grad_wqkv, grad_wout = pl.pallas_call(
        deliver,
        out_shape=shapes,
        in_specs=[vmem] * 4,
        out_specs=(hbm,) * 4,
        scratch_shapes=[sems(4)],
        compiler_params=pltpu.CompilerParams(vmem_limit_bytes=1024 * 1024),
    )(*results)
    return (mixed.T[None], grad_tokens.T[None], grad_wqkv, grad_wout)


def solution(mesh):
    in_specs = (P(None, "seq", None), P(None, "mp", None), P("mp", None), P(None, "seq", None))
    out_specs = (P(None, "seq", "mp"), P(None, "seq", "mp"), P("seq", None, "mp"), P("seq", "mp"))
    return jax.shard_map(shards, mesh=mesh, in_specs=in_specs, out_specs=out_specs, check_vma=False)
```
